32 devices in a mesh: group: 2 (over y), wide: 8 (over z, x), narrow: 2 (over core).
Axes of the slice: x: 2, y: 2, z: 4, core: 2. Of those that a mesh axis runs over, the one named last changes fastest.
Arguments:
- hidden_in: bfloat16 [16, 16384], P(('group', 'wide'), 'narrow'), parts along dimension 0, may hold values from -60 to 60
- norm_gain: float32 [16384], P('narrow'), may hold values from 0.1 to 1.9
- qkv_weight: bfloat16 [16384, 9216], P('narrow', 'wide'), may hold values from -0.046875 to 0.046875
- out_weight: bfloat16 [8192, 16384], P('narrow', 'wide'), may hold values from -0.25 to 0.25
- cache_keys: bfloat16 [16, 256, 512], P(('group', 'wide'), None, 'narrow'), parts along dimension 0, may hold values from -500 to 500
- cache_values: bfloat16 [16, 256, 512], P(('group', 'wide'), None, 'narrow'), parts along dimension 0, may hold values from -6 to 6
- cache_lengths: int32 [16], P(('group', 'wide')), parts along dimension 0, may hold values from 4 to 256, as said below
Outputs:
- layer_out: float32 [16, 16384], P(('group', 'wide'), 'narrow'), parts along dimension 0
The draws below stay inside these ranges and needn't reach their ends.
There are 2 independent parts, one for each index of `group`. The reference program is written for one: setup_inputs(seed, part) draws one part's arguments, and reference() takes and returns one part's arrays. A program takes and returns all parts, laid end to end along the dimension named above; an argument that names none is the same for every part. Nothing has to cross between parts.
Inputs may be any that keep to these rules, and one draw needn't show every extreme that they name: Some row's length is exactly 256 in every draw; row r's cached positions are 0 to cache_lengths[r] - 1 and its new token stands at position cache_lengths[r].
All inputs are finite; a program needn't handle non-finite values.
Results may differ from the reference program's by a relative error of at most 0.0058.
Values may be sent and summed in bfloat16 or wider, within the bound.
A program may use at most 64 MiB of HBM per device.

```python
import jax
import jax.numpy as jnp
from jax import lax

D = 16384
QH = 64
KVH = 4
HD = 128
CTX = 256
GQ = 16
COLS = 9216
ROWS = 8


def draw_cache_lengths(key, part):
    first_key, second_key = jax.random.split(jax.random.fold_in(key, 11))
    lengths = jax.random.randint(first_key, (ROWS,), 4, CTX + 1)
    longest = jax.random.randint(second_key, (), 0, ROWS)
    return jnp.where(jnp.arange(ROWS) == longest, CTX, lengths).astype(jnp.int32)


def draw_cache_keys(key, part):
    first_key = jax.random.fold_in(jax.random.fold_in(key, 23), 0)
    base = jnp.clip(jax.random.normal(first_key, (ROWS, CTX, KVH * HD), jnp.float32), -6.0, 6.0) * 2.5
    return base.astype(jnp.bfloat16)


def draw_hidden_in(key, part):
    first_key, second_key = jax.random.split(jax.random.fold_in(key, 37))
    spot = jnp.arange(D, dtype=jnp.float32) / (D - 1.0)
    column_scale = jnp.exp(jnp.log(0.3) + spot * jnp.log(10.0))
    values = jnp.clip(jax.random.normal(first_key, (ROWS, D), jnp.float32), -6.0, 6.0)
    row_scale = jnp.exp(jax.random.uniform(second_key, (ROWS, 1), jnp.float32, jnp.log(0.5), jnp.log(2.0)))
    return (values * column_scale[None, :] * row_scale).astype(jnp.bfloat16)


def block_scale(own_key, dims, pieces, smallest, high):
    def one(axis_at, shards_of):
        steps = jax.random.uniform(jax.random.fold_in(jax.random.fold_in(own_key, 6), axis_at), (shards_of,), jnp.float32, smallest / len(pieces), high / len(pieces))
        return jnp.repeat(jnp.exp(steps), dims[axis_at] // shards_of).reshape((-1,) + (1,) * (len(dims) - axis_at - 1))

    gain = one(*pieces[0])
    for cut in pieces[1:]:
        gain = gain * one(*cut)
    return gain


def normal_values(rng, dims, scale, most, cuts=(), kind=jnp.bfloat16):
    level = block_scale(rng, dims, cuts, -0.22, 0.18) if cuts else 1.0
    values = jax.random.normal(rng, dims, jnp.float32) * scale * level
    return jnp.minimum(jnp.maximum(values, -most), most).astype(kind)


def setup_inputs(seed: int = 0, part: int = 0) -> dict:
    splits = jax.random.split(jax.random.key(seed), 8)
    own_keys = jax.random.split(jax.random.fold_in(splits[7], part), 8)
    return {
        "hidden_in": draw_hidden_in(jax.random.fold_in(jax.random.fold_in(splits[7], part), 71), part),
        "norm_gain": jnp.clip(1.0 + 0.18 * jax.random.normal(splits[1], (D,), jnp.float32), 0.1, 1.9),
        "qkv_weight": normal_values(splits[2], (D, COLS), D ** -0.5, 0.046875, ((0, 2), (1, 8))),
        "out_weight": normal_values(splits[3], (QH * HD, D), (QH * HD // 16) ** -0.5, 0.25, ((0, 2), (1, 8))),
        "cache_keys": draw_cache_keys(jax.random.fold_in(jax.random.fold_in(splits[7], part), 71), part),
        "cache_values": normal_values(own_keys[5], (ROWS, CTX, KVH * HD), 1.0, 6.0, ((0, 8), (2, 2))),
        "cache_lengths": draw_cache_lengths(jax.random.fold_in(jax.random.fold_in(splits[7], part), 71), part),
    }


rope_theta = 500000.0
norm_eps = 1e-05

def rotary(values, position):
    half = values.shape[-1] // 2
    frequency = rope_theta ** (-jnp.arange(half, dtype=jnp.float32) * 2.0 / values.shape[-1])
    angles = position[..., None] * frequency
    cosine = jnp.cos(angles)
    sine = jnp.sin(angles)
    first = values[..., :half]
    second = values[..., half:]
    return jnp.concatenate([first * cosine - second * sine, second * cosine + first * sine], -1)

def attend_row(joined, keys, values, length):
    groups = joined.shape[0]
    share = joined.shape[1] - 2
    head_dim = joined.shape[2]
    position = length.astype(jnp.float32)
    query = (rotary(joined[:, :share], position) * head_dim ** (-0.5)).astype(jnp.bfloat16)
    new_key = rotary(joined[:, share], position).astype(jnp.bfloat16)
    new_value = joined[:, share + 1].astype(jnp.bfloat16)
    keys_four = keys.reshape(keys.shape[0], groups, head_dim).astype(jnp.float32)
    values_four = values.reshape(values.shape[0], groups, head_dim).astype(jnp.float32)
    scores = jnp.einsum('gjd,tgd->gjt', query.astype(jnp.float32), keys_four)
    own = lax.optimization_barrier(jnp.sum(query.astype(jnp.float32) * new_key.astype(jnp.float32)[:, None, :], -1))
    live = jnp.arange(keys.shape[0])[None, None, :] < length
    scores = jnp.where(live, scores, -1e+30)
    top = jnp.maximum(lax.optimization_barrier(jnp.max(scores, -1)), own)
    expo = jnp.exp(scores - top[..., None])
    own_expo = jnp.exp(own - top)
    total = lax.optimization_barrier(jnp.sum(expo, -1)) + own_expo
    probs = (expo / total[..., None]).astype(jnp.bfloat16)
    mixed = jnp.einsum('gjt,tgd->gjd', probs.astype(jnp.float32), values_four)
    mixed = mixed + (own_expo / total)[..., None] * new_value.astype(jnp.float32)[:, None, :]
    return mixed.astype(jnp.bfloat16).reshape(-1)

def reference(hidden_in, norm_gain, qkv_weight, out_weight, cache_keys, cache_values, cache_lengths):
    inputs = hidden_in.astype(jnp.float32)
    squares = lax.optimization_barrier(jnp.sum(inputs * inputs, -1))
    normed = (inputs * lax.rsqrt(squares / D + norm_eps)[:, None] * norm_gain).astype(jnp.bfloat16)
    joined = jnp.dot(normed, qkv_weight, preferred_element_type=jnp.float32)
    joined = joined.reshape(ROWS, KVH, GQ + 2, HD)

    def one_row(packed):
        return attend_row(packed[0], packed[1], packed[2], packed[3])
    mixed = lax.map(one_row, (joined, cache_keys, cache_values, cache_lengths))
    added = jnp.dot(mixed, out_weight, preferred_element_type=jnp.float32)
    return inputs + added
```

```python
import functools
import math

import jax
import jax.numpy as jnp
from jax import lax
from jax.experimental import pallas as pl
from jax.experimental.pallas import tpu as pltpu
from jax.sharding import PartitionSpec as P

HD = 128


rope_theta = 500000.0
norm_eps = 1e-05
MESH = pl.DeviceIdType.MESH


def chunks_of(depth):
    return max(1, depth // 512)


def decode_kernel(
    wide, narrow, heads, groups, features,
    h_hbm, g_hbm, len_ref, k_hbm, v_hbm, wq_hbm, wo_hbm, out_ref,
    h_in, gain, keys, values, wq, wo, hf, hrec, xs, lhs, ssrec, psend, prec, joined,
    mrec, ms, lhs2, osend, orec,
    in_sem, q_sem, w_sem, ss_s, ss_r, h_s, h_r, p_s, p_r, m_s, m_r, o_s, o_r,
):
    w = lax.axis_index("wide")
    n = lax.axis_index("narrow")
    peers = wide * narrow
    me = n * wide + w
    share = wide // narrow
    blocks = hf.shape[0]
    q_chunks, q_depth = wq.shape[0], wq.shape[1]
    w_chunks, w_depth = wo.shape[0], wo.shape[1]

    def load(c):
        return pltpu.make_async_copy(
            wq_hbm.at[pl.ds(pl.multiple_of(c * q_depth, q_depth), q_depth), :], wq.at[c], q_sem.at[c]
        )

    def load_out(c):
        return pltpu.make_async_copy(
            wo_hbm.at[pl.ds(pl.multiple_of(c * w_depth, w_depth), w_depth), :], wo.at[c], w_sem.at[c]
        )

    h_copy = pltpu.make_async_copy(h_hbm, h_in, in_sem.at[0])
    g_copy = pltpu.make_async_copy(g_hbm, gain, in_sem.at[1])
    k_copy = pltpu.make_async_copy(k_hbm, keys, in_sem.at[2])
    v_copy = pltpu.make_async_copy(v_hbm, values, in_sem.at[3])
    h_copy.start()
    g_copy.start()

    barrier = pltpu.get_barrier_semaphore()
    for d in range(1, peers):
        other = lax.rem(me + d, peers)
        pl.semaphore_signal(
            barrier, inc=1,
            device_id={"wide": lax.rem(other, wide), "narrow": other // wide},
            device_id_type=MESH,
        )

    @pl.loop(0, q_chunks)
    def _(c):
        load(c).start()

    h_copy.wait()
    wide_row = h_in[...].astype(jnp.float32)
    for b in range(blocks):
        hf[b : b + 1, :] = wide_row[:, b * HD : (b + 1) * HD]
    own = hf[...]
    ssrec[me] = jnp.sum(own * own, axis=0, keepdims=True)
    hrec[w] = own.astype(jnp.bfloat16)

    pl.semaphore_wait(barrier, peers - 1)

    ss_copies = []
    for d in range(1, peers):
        other = lax.rem(me + d, peers)
        copy = pltpu.make_async_remote_copy(
            src_ref=ssrec.at[me], dst_ref=ssrec.at[me],
            send_sem=ss_s.at[d], recv_sem=ss_r.at[me],
            device_id={"wide": lax.rem(other, wide), "narrow": other // wide},
            device_id_type=MESH,
        )
        copy.start()
        ss_copies.append(copy)

    def spread(buffer, send, recv):
        copies = []
        for d in range(1, wide):
            copy = pltpu.make_async_remote_copy(
                src_ref=buffer.at[w], dst_ref=buffer.at[w],
                send_sem=send.at[d], recv_sem=recv.at[w],
                device_id={"wide": lax.rem(w + d, wide)},
                device_id_type=MESH,
            )
            copy.start()
            copies.append(copy)
        return copies

    h_copies = spread(hrec, h_s, h_r)

    k_copy.start()
    v_copy.start()

    @pl.loop(0, w_chunks)
    def _(c):
        load_out(c).start()

    position = len_ref[0].astype(jnp.float32)
    lane = lax.broadcasted_iota(jnp.int32, (1, HD), 1)
    turn = lax.rem(lane, HD // 2).astype(jnp.float32)
    angles = position * jnp.exp(turn * (-2.0 / HD * math.log(rope_theta)))
    cosine = jnp.cos(angles)
    sine = jnp.where(lane < HD // 2, -jnp.sin(angles), jnp.sin(angles))

    g_copy.wait()
    gains = gain[...]
    for s in range(peers):
        @pl.when(s != me)
        def _():
            pltpu.make_async_copy(ssrec.at[s], ssrec.at[s], ss_r.at[s]).wait()
    squares = ssrec[0:wide]
    for part in range(1, narrow):
        squares = squares + ssrec[part * wide : (part + 1) * wide]
    scale = lax.rsqrt(jnp.sum(squares, axis=-1, keepdims=True) / features + norm_eps)

    for s in range(wide):
        @pl.when(s != w)
        def _():
            pltpu.make_async_copy(hrec.at[s], hrec.at[s], h_r.at[s]).wait()
        xs[s * blocks : (s + 1) * blocks, :] = hrec[s].astype(jnp.float32) * scale[s] * gains

    per = q_depth // HD
    for b in range(blocks):
        lhs[b // per, :, (b % per) * HD : (b % per + 1) * HD] = xs[
            pl.ds(b, wide, stride=blocks), :
        ].astype(jnp.bfloat16)

    def step(c, total):
        load(c).wait()
        return total + jnp.dot(lhs[c], wq[c], preferred_element_type=jnp.float32)

    total = lax.fori_loop(0, q_chunks, step, jnp.zeros((wide, heads * HD), jnp.float32))
    for j in range(heads):
        psend[:, j, :] = total[:, j * HD : (j + 1) * HD]

    slot = lax.rem(w, share) * narrow + n
    owner = w // share

    def collect(source, target, send, recv):
        copies = []
        for d in range(wide):
            row = lax.rem(w + d, wide)
            copy = pltpu.make_async_remote_copy(
                src_ref=source.at[row], dst_ref=target.at[slot],
                send_sem=send.at[d], recv_sem=recv.at[slot],
                device_id={"wide": row, "narrow": owner},
                device_id_type=MESH,
            )
            if d == 0:
                @pl.when(owner == n)
                def _():
                    pltpu.make_async_copy(source.at[w], target.at[slot], recv.at[slot]).start()

                @pl.when(owner != n)
                def _():
                    copy.start()
            else:
                copy.start()
            copies.append(copy)
        for s in range(wide):
            pltpu.make_async_copy(target.at[s], target.at[s], recv.at[s]).wait()
        return copies

    p_copies = collect(psend, prec, p_s, p_r)

    k_copy.wait()
    v_copy.wait()
    per_group = share // groups
    context = keys.shape[1]
    queries = per_group * heads - 2
    for g in range(groups):
        for b in range(per_group):
            at = (g * per_group + b) * narrow
            block = prec[at]
            for part in range(1, narrow):
                block = block + prec[at + part]
            joined[g, b * heads : (b + 1) * heads, :] = block
        turned = joined[g, 0 : queries, :]
        turned = turned * cosine + pltpu.roll(turned, HD // 2, 1) * sine
        query = (turned * HD ** (-0.5)).astype(jnp.bfloat16)
        new_key = joined[g, queries : queries + 1, :]
        new_key = new_key * cosine + pltpu.roll(new_key, HD // 2, 1) * sine
        new_key = new_key.astype(jnp.bfloat16).astype(jnp.float32)
        new_value = joined[g, queries + 1 : queries + 2, :].astype(jnp.bfloat16).astype(jnp.float32)
        scores = lax.dot_general(
            query, keys[0, :, g * HD : (g + 1) * HD], (((1,), (1,)), ((), ())),
            preferred_element_type=jnp.float32,
        )
        own_score = jnp.sum(query.astype(jnp.float32) * new_key, axis=-1, keepdims=True)
        live = lax.broadcasted_iota(jnp.int32, (queries, context), 1) < len_ref[0]
        scores = jnp.where(live, scores, -1e30)
        top = jnp.maximum(jnp.max(scores, axis=-1, keepdims=True), own_score)
        expo = jnp.exp(scores - top)
        own_expo = jnp.exp(own_score - top)
        weight = jnp.sum(expo, axis=-1, keepdims=True) + own_expo
        probs = (expo / weight).astype(jnp.bfloat16)
        mixed = jnp.dot(
            probs, values[0, :, g * HD : (g + 1) * HD], preferred_element_type=jnp.float32
        )
        mixed = mixed + (own_expo / weight) * new_value
        mrec[w, g * queries : (g + 1) * queries, :] = mixed.astype(jnp.bfloat16)

    m_copies = spread(mrec, m_s, m_r)
    rows = mrec.shape[1]
    for s in range(wide):
        @pl.when(s != w)
        def _():
            pltpu.make_async_copy(mrec.at[s], mrec.at[s], m_r.at[s]).wait()
        ms[s * rows : (s + 1) * rows, :] = mrec[s].astype(jnp.float32)
    per = w_depth // HD
    for b in range(rows):
        lhs2[b // per, :, (b % per) * HD : (b % per + 1) * HD] = ms[
            pl.ds(b, wide, stride=rows), :
        ].astype(jnp.bfloat16)

    def step_out(c, total):
        load_out(c).wait()
        return total + jnp.dot(lhs2[c], wo[c], preferred_element_type=jnp.float32)

    out_blocks = osend.shape[1]
    total = lax.fori_loop(0, w_chunks, step_out, jnp.zeros((wide, out_blocks * HD), jnp.float32))
    for j in range(out_blocks):
        osend[:, j, :] = total[:, j * HD : (j + 1) * HD]

    o_copies = collect(osend, orec, o_s, o_r)
    for b in range(share):
        block = orec[b * narrow]
        for part in range(1, narrow):
            block = block + orec[b * narrow + part]
        at = slice(b * out_blocks, (b + 1) * out_blocks)
        out_ref[at, :] = hf[at, :] + block

    for copy in ss_copies + h_copies + m_copies:
        copy.wait_send()
    for copies in (p_copies, o_copies):
        for copy in copies[1:]:
            copy.wait_send()

        @pl.when(owner != n)
        def _():
            copies[0].wait_send()


def fused(wide, narrow, hidden_in, norm_gain, qkv_weight, out_weight, cache_keys, cache_values, cache_lengths):
    depth, columns = qkv_weight.shape
    out_depth, out_columns = out_weight.shape
    heads = columns // HD
    groups = cache_keys.shape[2] // HD
    blocks = depth // HD
    rows = out_depth // HD
    out_blocks = out_columns // HD
    share = wide // narrow
    q_chunks = chunks_of(depth)
    w_chunks = chunks_of(out_depth)
    bf16, f32 = jnp.bfloat16, jnp.float32
    dma = pltpu.SemaphoreType.DMA
    anywhere = pl.BlockSpec(memory_space=pl.ANY)
    out = pl.pallas_call(
        functools.partial(decode_kernel, wide, narrow, heads, groups, depth * narrow),
        out_shape=jax.ShapeDtypeStruct((blocks, HD), f32),
        in_specs=[
            anywhere, anywhere, pl.BlockSpec(memory_space=pltpu.SMEM),
            anywhere, anywhere, anywhere, anywhere,
        ],
        out_specs=pl.BlockSpec(memory_space=pltpu.VMEM),
        scratch_shapes=[
            pltpu.VMEM(hidden_in.shape, bf16),
            pltpu.VMEM((blocks, HD), f32),
            pltpu.VMEM(cache_keys.shape, bf16),
            pltpu.VMEM(cache_values.shape, bf16),
            pltpu.VMEM((q_chunks, depth // q_chunks, columns), bf16),
            pltpu.VMEM((w_chunks, out_depth // w_chunks, out_columns), bf16),
            pltpu.VMEM((blocks, HD), f32),
            pltpu.VMEM((wide, blocks, HD), bf16),
            pltpu.VMEM((wide * blocks, HD), f32),
            pltpu.VMEM((q_chunks, wide, depth // q_chunks), bf16),
            pltpu.VMEM((wide * narrow, 1, HD), f32),
            pltpu.VMEM((wide, heads, HD), f32),
            pltpu.VMEM((wide, heads, HD), f32),
            pltpu.VMEM((groups, share // groups * heads, HD), f32),
            pltpu.VMEM((wide, rows, HD), bf16),
            pltpu.VMEM((wide * rows, HD), f32),
            pltpu.VMEM((w_chunks, wide, out_depth // w_chunks), bf16),
            pltpu.VMEM((wide, out_blocks, HD), f32),
            pltpu.VMEM((wide, out_blocks, HD), f32),
            dma((4,)), dma((q_chunks,)), dma((w_chunks,)),
            dma((wide * narrow,)), dma((wide * narrow,)),
            dma((wide,)), dma((wide,)),
            dma((wide,)), dma((wide,)),
            dma((wide,)), dma((wide,)),
            dma((wide,)), dma((wide,)),
        ],
        compiler_params=pltpu.CompilerParams(
            collective_id=0, has_side_effects=True, vmem_limit_bytes=52 * 1024 * 1024
        ),
        cost_estimate=pl.CostEstimate(
            flops=2 * wide * (depth * columns + out_depth * out_columns),
            bytes_accessed=2 * (depth * columns + out_depth * out_columns),
            transcendentals=0,
        ),
        name="decode",
    )(
        hidden_in, norm_gain.reshape(blocks, HD), cache_lengths,
        cache_keys, cache_values, qkv_weight, out_weight,
    )
    return out.reshape(1, blocks * HD)


def fits(wide, narrow, hidden_in, qkv_weight, out_weight, cache_keys):
    columns = qkv_weight.shape[1]
    groups = cache_keys.shape[2] // HD
    if hidden_in.shape[0] != 1 or columns % HD or out_weight.shape[1] % (16 * HD):
        return False
    if wide % narrow or (wide // narrow) % groups:
        return False
    if qkv_weight.shape[0] % 2048 or out_weight.shape[0] % 2048:
        return False
    queries = (wide // narrow) // groups * (columns // HD) - 2
    return queries * groups * HD == out_weight.shape[0]


def rotary(values, position):
    half = values.shape[-1] // 2
    frequency = rope_theta ** (-jnp.arange(half, dtype=jnp.float32) * 2.0 / values.shape[-1])
    angles = position[..., None] * frequency
    cosine = jnp.cos(angles)
    sine = jnp.sin(angles)
    first = values[..., :half]
    second = values[..., half:]
    return jnp.concatenate([first * cosine - second * sine, second * cosine + first * sine], -1)


def attend(joined, keys, values, lengths):
    count = joined.shape[0]
    groups = joined.shape[1]
    share = joined.shape[2] - 2
    head_dim = joined.shape[3]
    capacity = keys.shape[1]
    position = lengths.astype(jnp.float32)
    query = (rotary(joined[:, :, :share], position[:, None, None]) * head_dim ** (-0.5)).astype(
        jnp.bfloat16
    )
    new_key = rotary(joined[:, :, share], position[:, None]).astype(jnp.bfloat16)
    new_value = joined[:, :, share + 1].astype(jnp.bfloat16)
    keys_four = keys.reshape(count, capacity, groups, head_dim)
    values_four = values.reshape(count, capacity, groups, head_dim)
    scores = jnp.einsum("bgjd,btgd->bgjt", query, keys_four, preferred_element_type=jnp.float32)
    own = jnp.sum(query.astype(jnp.float32) * new_key.astype(jnp.float32)[:, :, None, :], -1)
    live = jnp.arange(capacity)[None, None, None, :] < lengths[:, None, None, None]
    scores = jnp.where(live, scores, -1e30)
    top = jnp.maximum(jnp.max(scores, -1), own)
    expo = jnp.exp(scores - top[..., None])
    own_expo = jnp.exp(own - top)
    total = jnp.sum(expo, -1) + own_expo
    probs = (expo / total[..., None]).astype(jnp.bfloat16)
    mixed = jnp.einsum("bgjt,btgd->bgjd", probs, values_four, preferred_element_type=jnp.float32)
    mixed = mixed + (own_expo / total)[..., None] * new_value.astype(jnp.float32)[:, :, None, :]
    return mixed.astype(jnp.bfloat16).reshape(count, groups * share * head_dim)


def body(hidden_in, norm_gain, qkv_weight, out_weight, cache_keys, cache_values, cache_lengths):
    wide, narrow = lax.axis_size("wide"), lax.axis_size("narrow")
    if fits(wide, narrow, hidden_in, qkv_weight, out_weight, cache_keys):
        return fused(
            wide, narrow, hidden_in, norm_gain, qkv_weight, out_weight,
            cache_keys, cache_values, cache_lengths,
        )
    inputs = hidden_in.astype(jnp.float32)
    row_count = hidden_in.shape[0]
    squares = lax.psum(jnp.sum(inputs * inputs, -1), "narrow")
    normed = (inputs * lax.rsqrt(squares / (hidden_in.shape[1] * narrow) + norm_eps)[:, None] * norm_gain).astype(jnp.bfloat16)
    partial_qkv = jnp.dot(
        lax.all_gather(normed, "wide", axis=0, tiled=True),
        qkv_weight,
        preferred_element_type=jnp.float32,
    )
    all_rows, col_block = partial_qkv.shape
    halves = partial_qkv.reshape(all_rows, 1, 2, col_block // 2)
    paired = lax.psum_scatter(halves, "narrow", scatter_dimension=2, tiled=True)
    moved = lax.all_to_all(paired, "wide", split_axis=0, concat_axis=1, tiled=True)
    blocks = moved.shape[1]
    parted = moved.reshape(row_count, 2, blocks // 2, 1, col_block // 2)
    owned = lax.all_to_all(parted, "narrow", split_axis=1, concat_axis=3, tiled=True)
    owned = owned.reshape(row_count, blocks // 2 * col_block)
    groups = cache_keys.shape[2] // HD
    owned = owned.reshape(row_count, groups, owned.shape[1] // (groups * HD), HD)
    mixed = attend(owned, cache_keys, cache_values, cache_lengths)
    partial_out = jnp.dot(
        lax.all_gather(mixed, "wide", axis=0, tiled=True),
        out_weight,
        preferred_element_type=jnp.float32,
    )
    all_rows, col_block = partial_out.shape
    halves = partial_out.reshape(all_rows, 1, 2, col_block // 2)
    paired = lax.psum_scatter(halves, "narrow", scatter_dimension=2, tiled=True)
    moved = lax.all_to_all(paired, "wide", split_axis=0, concat_axis=1, tiled=True)
    blocks = moved.shape[1]
    parted = moved.reshape(row_count, 2, blocks // 2, 1, col_block // 2)
    added = lax.all_to_all(parted, "narrow", split_axis=1, concat_axis=3, tiled=True)
    added = added.reshape(row_count, blocks // 2 * col_block)
    return inputs + added


def solution(mesh):
    placed = (
        P(("group", "wide"), "narrow"),
        P("narrow"),
        P("narrow", "wide"),
        P("narrow", "wide"),
        P(("group", "wide"), None, "narrow"),
        P(("group", "wide"), None, "narrow"),
        P(("group", "wide")),
    )
    return jax.shard_map(
        body, mesh=mesh, in_specs=placed, out_specs=P(("group", "wide"), "narrow"), check_vma=False
    )
```

```python
import functools
import math

import jax
import jax.numpy as jnp
from jax import lax
from jax.experimental import pallas as pl
from jax.experimental.pallas import tpu as pltpu
from jax.sharding import PartitionSpec as P

HD = 128


rope_theta = 500000.0
norm_eps = 1e-05
MESH = pl.DeviceIdType.MESH


PARTS = 2
PIECE = 512
STEP = 2048


def decode_kernel(
    wide, narrow, heads, groups, features,
    h_hbm, g_hbm, len_ref, k_hbm, v_hbm, wq_hbm, wo_hbm, out_ref,
    h_in, gain, keys, values, wq, wo, hf, hrec, xs, lhs, ssrec, psend, prec, joined,
    mrec, ms, lhs2, osend, orec,
    in_sem, q_sem, w_sem, ss_s, ss_r, h_s, h_r, p_s, p_r, m_s, m_r, o_s, o_r,
):
    w = lax.axis_index("wide")
    n = lax.axis_index("narrow")
    peers = wide * narrow
    me = n * wide + w
    share = wide // narrow
    blocks = hf.shape[0]

    def piece(c):
        return pl.ds(pl.multiple_of(c * PIECE, PIECE), PIECE)

    def load(c):
        return pltpu.make_async_copy(wq_hbm.at[piece(c), :], wq.at[piece(c), :], q_sem.at[c])

    def load_out(c):
        return pltpu.make_async_copy(wo_hbm.at[piece(c), :], wo.at[piece(c), :], w_sem.at[c])

    h_copy = pltpu.make_async_copy(h_hbm, h_in, in_sem.at[0])
    g_copy = pltpu.make_async_copy(g_hbm, gain, in_sem.at[1])
    k_copy = pltpu.make_async_copy(k_hbm, keys, in_sem.at[2])
    v_copy = pltpu.make_async_copy(v_hbm, values, in_sem.at[3])
    h_copy.start()
    g_copy.start()

    barrier = pltpu.get_barrier_semaphore()
    for d in range(1, peers):
        other = lax.rem(me + d, peers)
        pl.semaphore_signal(
            barrier, inc=1,
            device_id={"wide": lax.rem(other, wide), "narrow": other // wide},
            device_id_type=MESH,
        )

    @pl.loop(0, wq.shape[0] // PIECE)
    def _(c):
        load(c).start()

    h_copy.wait()
    wide_row = h_in[...].astype(jnp.float32)
    for b in range(blocks):
        hf[b : b + 1, :] = wide_row[:, b * HD : (b + 1) * HD]
    own = hf[...]
    ssrec[me] = jnp.sum(own * own, axis=0, keepdims=True)
    hrec[w] = own.astype(jnp.bfloat16)

    pl.semaphore_wait(barrier, peers - 1)

    ss_copies = []
    for d in range(1, peers):
        other = lax.rem(me + d, peers)
        copy = pltpu.make_async_remote_copy(
            src_ref=ssrec.at[me], dst_ref=ssrec.at[me],
            send_sem=ss_s.at[d], recv_sem=ss_r.at[me],
            device_id={"wide": lax.rem(other, wide), "narrow": other // wide},
            device_id_type=MESH,
        )
        copy.start()
        ss_copies.append(copy)

    def spread(buffer, part, size, send, recv):
        copies = []
        block = buffer.at[w, pl.ds(part * size, size)]
        for d in range(1, wide):
            copy = pltpu.make_async_remote_copy(
                src_ref=block, dst_ref=block,
                send_sem=send.at[part, d], recv_sem=recv.at[part, w],
                device_id={"wide": lax.rem(w + d, wide)},
                device_id_type=MESH,
            )
            copy.start()
            copies.append(copy)
        return copies

    half = blocks // PARTS
    h_copies = []
    for part in range(PARTS):
        h_copies += spread(hrec, part, half, h_s, h_r)

    k_copy.start()
    v_copy.start()

    @pl.loop(0, wo.shape[0] // PIECE)
    def _(c):
        load_out(c).start()

    position = len_ref[0].astype(jnp.float32)
    lane = lax.broadcasted_iota(jnp.int32, (1, HD), 1)
    turn = lax.rem(lane, HD // 2).astype(jnp.float32)
    angles = position * jnp.exp(turn * (-2.0 / HD * math.log(rope_theta)))
    cosine = jnp.cos(angles)
    sine = jnp.where(lane < HD // 2, -jnp.sin(angles), jnp.sin(angles))

    g_copy.wait()
    gains = gain[...]
    for s in range(peers):
        @pl.when(s != me)
        def _():
            pltpu.make_async_copy(ssrec.at[s], ssrec.at[s], ss_r.at[s]).wait()
    squares = ssrec[0:wide]
    for part in range(1, narrow):
        squares = squares + ssrec[part * wide : (part + 1) * wide]
    scale = lax.rsqrt(jnp.sum(squares, axis=-1, keepdims=True) / features + norm_eps)

    def arrive(buffer, part, size, s, recv):
        block = buffer.at[s, pl.ds(part * size, size)]

        @pl.when(s != w)
        def _():
            pltpu.make_async_copy(block, block, recv.at[part, s]).wait()

    total = jnp.zeros((wide, heads * HD), jnp.float32)
    steps = wq.shape[0] // PARTS // STEP
    per = STEP // HD
    for part in range(PARTS):
        first = part * half
        for s in range(wide):
            arrive(hrec, part, half, s, h_r)
            xs[s * half : (s + 1) * half, :] = (
                hrec[s, first : first + half, :].astype(jnp.float32)
                * scale[s] * gains[first : first + half, :]
            )
        for b in range(half):
            lhs[b // per, :, (b % per) * HD : (b % per + 1) * HD] = xs[
                pl.ds(b, wide, stride=half), :
            ].astype(jnp.bfloat16)

        def step(c, total):
            at = part * steps + c
            for i in range(STEP // PIECE):
                load(at * (STEP // PIECE) + i).wait()
            block = wq[pl.ds(pl.multiple_of(at * STEP, STEP), STEP), :]
            return total + jnp.dot(lhs[c], block, preferred_element_type=jnp.float32)

        total = lax.fori_loop(0, steps, step, total)
    for j in range(heads):
        psend[:, j, :] = total[:, j * HD : (j + 1) * HD]

    slot = lax.rem(w, share) * narrow + n
    owner = w // share

    def collect(source, target, send, recv):
        copies = []
        for d in range(wide):
            row = lax.rem(w + d, wide)
            copy = pltpu.make_async_remote_copy(
                src_ref=source.at[row], dst_ref=target.at[slot],
                send_sem=send.at[d], recv_sem=recv.at[slot],
                device_id={"wide": row, "narrow": owner},
                device_id_type=MESH,
            )
            if d == 0:
                @pl.when(owner == n)
                def _():
                    pltpu.make_async_copy(source.at[w], target.at[slot], recv.at[slot]).start()

                @pl.when(owner != n)
                def _():
                    copy.start()
            else:
                copy.start()
            copies.append(copy)
        return copies

    def receive(target, recv):
        for s in range(wide):
            pltpu.make_async_copy(target.at[s], target.at[s], recv.at[s]).wait()

    p_copies = collect(psend, prec, p_s, p_r)
    receive(prec, p_r)

    k_copy.wait()
    v_copy.wait()
    per_group = share // groups
    context = keys.shape[1]
    queries = per_group * heads - 2
    m_copies = []
    for g in range(groups):
        for b in range(per_group):
            at = (g * per_group + b) * narrow
            block = prec[at]
            for part in range(1, narrow):
                block = block + prec[at + part]
            joined[g, b * heads : (b + 1) * heads, :] = block
        turned = joined[g, 0 : queries, :]
        turned = turned * cosine + pltpu.roll(turned, HD // 2, 1) * sine
        query = (turned * HD ** (-0.5)).astype(jnp.bfloat16)
        new_key = joined[g, queries : queries + 1, :]
        new_key = new_key * cosine + pltpu.roll(new_key, HD // 2, 1) * sine
        new_key = new_key.astype(jnp.bfloat16).astype(jnp.float32)
        new_value = joined[g, queries + 1 : queries + 2, :].astype(jnp.bfloat16).astype(jnp.float32)
        scores = lax.dot_general(
            query, keys[0, :, g * HD : (g + 1) * HD], (((1,), (1,)), ((), ())),
            preferred_element_type=jnp.float32,
        )
        own_score = jnp.sum(query.astype(jnp.float32) * new_key, axis=-1, keepdims=True)
        live = lax.broadcasted_iota(jnp.int32, (queries, context), 1) < len_ref[0]
        scores = jnp.where(live, scores, -1e30)
        top = jnp.maximum(jnp.max(scores, axis=-1, keepdims=True), own_score)
        expo = jnp.exp(scores - top)
        own_expo = jnp.exp(own_score - top)
        weight = jnp.sum(expo, axis=-1, keepdims=True) + own_expo
        probs = (expo / weight).astype(jnp.bfloat16)
        mixed = jnp.dot(
            probs, values[0, :, g * HD : (g + 1) * HD], preferred_element_type=jnp.float32
        )
        mixed = mixed + (own_expo / weight) * new_value
        mrec[w, g * queries : (g + 1) * queries, :] = mixed.astype(jnp.bfloat16)

        m_copies += spread(mrec, g, queries, m_s, m_r)

    columns = wo.shape[1]
    width = columns // PARTS
    deep = queries * HD
    o_copies = []
    total = None
    for g in range(groups):
        for s in range(wide):
            arrive(mrec, g, queries, s, m_r)
            ms[s * queries : (s + 1) * queries, :] = mrec[
                s, g * queries : (g + 1) * queries, :
            ].astype(jnp.float32)
        for b in range(queries):
            lhs2[:, b * HD : (b + 1) * HD] = ms[
                pl.ds(b, wide, stride=queries), :
            ].astype(jnp.bfloat16)
        for i in range(deep // PIECE):
            load_out(g * (deep // PIECE) + i).wait()
        mine = lhs2[...]
        if g < groups - 1:
            product = jnp.dot(
                mine, wo[g * deep : (g + 1) * deep, :], preferred_element_type=jnp.float32
            )
            total = product if total is None else total + product
            continue
        for part in range(PARTS):
            at = slice(part * width, (part + 1) * width)
            product = jnp.dot(
                mine, wo[g * deep : (g + 1) * deep, at], preferred_element_type=jnp.float32
            )
            if total is not None:
                product = total[:, at] + product
            for j in range(width // HD):
                osend[part, :, j, :] = product[:, j * HD : (j + 1) * HD]
            o_copies.append(
                collect(osend.at[part], orec.at[part], o_s.at[part], o_r.at[part])
            )

    count = width // HD
    for part in range(PARTS):
        receive(orec.at[part], o_r.at[part])
        for b in range(share):
            block = orec[part, b * narrow]
            for i in range(1, narrow):
                block = block + orec[part, b * narrow + i]
            start = b * (columns // HD) + part * count
            out_ref[start : start + count, :] = hf[start : start + count, :] + block

    for copy in ss_copies + h_copies + m_copies:
        copy.wait_send()
    for copies in [p_copies] + o_copies:
        for copy in copies[1:]:
            copy.wait_send()

        @pl.when(owner != n)
        def _():
            copies[0].wait_send()


def fused(wide, narrow, hidden_in, norm_gain, qkv_weight, out_weight, cache_keys, cache_values, cache_lengths):
    depth, columns = qkv_weight.shape
    out_depth, out_columns = out_weight.shape
    heads = columns // HD
    groups = cache_keys.shape[2] // HD
    blocks = depth // HD
    rows = out_depth // HD
    out_blocks = out_columns // HD
    share = wide // narrow
    queries = rows // groups
    bf16, f32 = jnp.bfloat16, jnp.float32
    dma = pltpu.SemaphoreType.DMA
    anywhere = pl.BlockSpec(memory_space=pltpu.HBM)
    out = pl.pallas_call(
        functools.partial(decode_kernel, wide, narrow, heads, groups, depth * narrow),
        out_shape=jax.ShapeDtypeStruct((blocks, HD), f32),
        in_specs=[
            anywhere, anywhere, pl.BlockSpec(memory_space=pltpu.SMEM),
            anywhere, anywhere, anywhere, anywhere,
        ],
        out_specs=pl.BlockSpec(memory_space=pltpu.VMEM),
        scratch_shapes=[
            pltpu.VMEM(hidden_in.shape, bf16),
            pltpu.VMEM((blocks, HD), f32),
            pltpu.VMEM(cache_keys.shape, bf16),
            pltpu.VMEM(cache_values.shape, bf16),
            pltpu.VMEM((depth, columns), bf16),
            pltpu.VMEM((out_depth, out_columns), bf16),
            pltpu.VMEM((blocks, HD), f32),
            pltpu.VMEM((wide, blocks, HD), bf16),
            pltpu.VMEM((wide * blocks // PARTS, HD), f32),
            pltpu.VMEM((depth // PARTS // STEP, wide, STEP), bf16),
            pltpu.VMEM((wide * narrow, 1, HD), f32),
            pltpu.VMEM((wide, heads, HD), f32),
            pltpu.VMEM((wide, heads, HD), f32),
            pltpu.VMEM((groups, share // groups * heads, HD), f32),
            pltpu.VMEM((wide, rows, HD), bf16),
            pltpu.VMEM((wide * queries, HD), f32),
            pltpu.VMEM((wide, queries * HD), bf16),
            pltpu.VMEM((PARTS, wide, out_blocks // PARTS, HD), f32),
            pltpu.VMEM((PARTS, wide, out_blocks // PARTS, HD), f32),
            dma((4,)), dma((depth // PIECE,)), dma((out_depth // PIECE,)),
            dma((wide * narrow,)), dma((wide * narrow,)),
            dma((PARTS, wide)), dma((PARTS, wide)),
            dma((wide,)), dma((wide,)),
            dma((groups, wide)), dma((groups, wide)),
            dma((PARTS, wide)), dma((PARTS, wide)),
        ],
        compiler_params=pltpu.CompilerParams(
            collective_id=0, has_side_effects=True, vmem_limit_bytes=63 * 1024 * 1024 + 768 * 1024
        ),
        cost_estimate=pl.CostEstimate(
            flops=2 * wide * (depth * columns + out_depth * out_columns),
            bytes_accessed=2 * (depth * columns + out_depth * out_columns),
            transcendentals=0,
        ),
        name="decode",
    )(
        hidden_in, norm_gain.reshape(blocks, HD), cache_lengths,
        cache_keys, cache_values, qkv_weight, out_weight,
    )
    return out.reshape(1, blocks * HD)


def fits(wide, narrow, hidden_in, qkv_weight, out_weight, cache_keys):
    columns = qkv_weight.shape[1]
    groups = cache_keys.shape[2] // HD
    if hidden_in.shape[0] != 1 or columns % HD or out_weight.shape[1] % (16 * HD):
        return False
    if wide % narrow or (wide // narrow) % groups:
        return False
    queries = (wide // narrow) // groups * (columns // HD) - 2
    if qkv_weight.shape[0] % (PARTS * STEP) or queries * HD % PIECE or queries % 16:
        return False
    return queries * groups * HD == out_weight.shape[0]


def rotary(values, position):
    half = values.shape[-1] // 2
    frequency = rope_theta ** (-jnp.arange(half, dtype=jnp.float32) * 2.0 / values.shape[-1])
    angles = position[..., None] * frequency
    cosine = jnp.cos(angles)
    sine = jnp.sin(angles)
    first = values[..., :half]
    second = values[..., half:]
    return jnp.concatenate([first * cosine - second * sine, second * cosine + first * sine], -1)


def attend(joined, keys, values, lengths):
    count = joined.shape[0]
    groups = joined.shape[1]
    share = joined.shape[2] - 2
    head_dim = joined.shape[3]
    capacity = keys.shape[1]
    position = lengths.astype(jnp.float32)
    query = (rotary(joined[:, :, :share], position[:, None, None]) * head_dim ** (-0.5)).astype(
        jnp.bfloat16
    )
    new_key = rotary(joined[:, :, share], position[:, None]).astype(jnp.bfloat16)
    new_value = joined[:, :, share + 1].astype(jnp.bfloat16)
    keys_four = keys.reshape(count, capacity, groups, head_dim)
    values_four = values.reshape(count, capacity, groups, head_dim)
    scores = jnp.einsum("bgjd,btgd->bgjt", query, keys_four, preferred_element_type=jnp.float32)
    own = jnp.sum(query.astype(jnp.float32) * new_key.astype(jnp.float32)[:, :, None, :], -1)
    live = jnp.arange(capacity)[None, None, None, :] < lengths[:, None, None, None]
    scores = jnp.where(live, scores, -1e30)
    top = jnp.maximum(jnp.max(scores, -1), own)
    expo = jnp.exp(scores - top[..., None])
    own_expo = jnp.exp(own - top)
    total = jnp.sum(expo, -1) + own_expo
    probs = (expo / total[..., None]).astype(jnp.bfloat16)
    mixed = jnp.einsum("bgjt,btgd->bgjd", probs, values_four, preferred_element_type=jnp.float32)
    mixed = mixed + (own_expo / total)[..., None] * new_value.astype(jnp.float32)[:, :, None, :]
    return mixed.astype(jnp.bfloat16).reshape(count, groups * share * head_dim)


def body(hidden_in, norm_gain, qkv_weight, out_weight, cache_keys, cache_values, cache_lengths):
    wide, narrow = lax.axis_size("wide"), lax.axis_size("narrow")
    if fits(wide, narrow, hidden_in, qkv_weight, out_weight, cache_keys):
        return fused(
            wide, narrow, hidden_in, norm_gain, qkv_weight, out_weight,
            cache_keys, cache_values, cache_lengths,
        )
    inputs = hidden_in.astype(jnp.float32)
    row_count = hidden_in.shape[0]
    squares = lax.psum(jnp.sum(inputs * inputs, -1), "narrow")
    normed = (inputs * lax.rsqrt(squares / (hidden_in.shape[1] * narrow) + norm_eps)[:, None] * norm_gain).astype(jnp.bfloat16)
    partial_qkv = jnp.dot(
        lax.all_gather(normed, "wide", axis=0, tiled=True),
        qkv_weight,
        preferred_element_type=jnp.float32,
    )
    all_rows, col_block = partial_qkv.shape
    halves = partial_qkv.reshape(all_rows, 1, 2, col_block // 2)
    paired = lax.psum_scatter(halves, "narrow", scatter_dimension=2, tiled=True)
    moved = lax.all_to_all(paired, "wide", split_axis=0, concat_axis=1, tiled=True)
    blocks = moved.shape[1]
    parted = moved.reshape(row_count, 2, blocks // 2, 1, col_block // 2)
    owned = lax.all_to_all(parted, "narrow", split_axis=1, concat_axis=3, tiled=True)
    owned = owned.reshape(row_count, blocks // 2 * col_block)
    groups = cache_keys.shape[2] // HD
    owned = owned.reshape(row_count, groups, owned.shape[1] // (groups * HD), HD)
    mixed = attend(owned, cache_keys, cache_values, cache_lengths)
    partial_out = jnp.dot(
        lax.all_gather(mixed, "wide", axis=0, tiled=True),
        out_weight,
        preferred_element_type=jnp.float32,
    )
    all_rows, col_block = partial_out.shape
    halves = partial_out.reshape(all_rows, 1, 2, col_block // 2)
    paired = lax.psum_scatter(halves, "narrow", scatter_dimension=2, tiled=True)
    moved = lax.all_to_all(paired, "wide", split_axis=0, concat_axis=1, tiled=True)
    blocks = moved.shape[1]
    parted = moved.reshape(row_count, 2, blocks // 2, 1, col_block // 2)
    added = lax.all_to_all(parted, "narrow", split_axis=1, concat_axis=3, tiled=True)
    added = added.reshape(row_count, blocks // 2 * col_block)
    return inputs + added


def solution(mesh):
    placed = (
        P(("group", "wide"), "narrow"),
        P("narrow"),
        P("narrow", "wide"),
        P("narrow", "wide"),
        P(("group", "wide"), None, "narrow"),
        P(("group", "wide"), None, "narrow"),
        P(("group", "wide")),
    )
    return jax.shard_map(
        body, mesh=mesh, in_specs=placed, out_specs=P(("group", "wide"), "narrow"), check_vma=False
    )
```

```python
import functools
import math

import jax
import jax.numpy as jnp
from jax import lax
from jax.experimental import pallas as pl
from jax.experimental.pallas import tpu as pltpu
from jax.sharding import PartitionSpec as P

HD = 128


rope_theta = 500000.0
norm_eps = 1e-05
MESH = pl.DeviceIdType.MESH


PARTS = 2
PIECE = 512
STEP = 2048


def decode_kernel(
    ways, wide, narrow, heads, groups, features,
    h_hbm, g_hbm, len_ref, k_hbm, v_hbm, wq_hbm, wo_hbm, out_ref,
    h_in, gain, keys, values, wq, wo, hf, hsend, hrec, xs, lhs, ssown, ssrec, psend, prec, joined,
    msend, mrec, ms, lhs2, osend, orec,
    in_sem, q_sem, w_sem, ss_s, ss_r, h_s, h_r, p_s, p_r, m_s, m_r, o_s, o_r,
):
    y = lax.axis_index("group")
    w = lax.axis_index("wide")
    n = lax.axis_index("narrow")
    rows = ways * wide
    me = y * wide + w
    share = wide // narrow
    blocks = hf.shape[0]
    depth, out_depth = wq.shape[0], wo.shape[0]

    def load(c):
        at = pl.multiple_of(y * depth + c * PIECE, PIECE)
        to = pl.multiple_of(c * PIECE, PIECE)
        return pltpu.make_async_copy(
            wq_hbm.at[pl.ds(at, PIECE), :], wq.at[pl.ds(to, PIECE), :], q_sem.at[c]
        )

    def load_out(c):
        at = pl.multiple_of(y * out_depth + c * PIECE, PIECE)
        to = pl.multiple_of(c * PIECE, PIECE)
        return pltpu.make_async_copy(
            wo_hbm.at[pl.ds(at, PIECE), :], wo.at[pl.ds(to, PIECE), :], w_sem.at[c]
        )

    h_copy = pltpu.make_async_copy(h_hbm, h_in, in_sem.at[0])
    g_copy = pltpu.make_async_copy(g_hbm, gain, in_sem.at[1])
    k_copy = pltpu.make_async_copy(k_hbm, keys, in_sem.at[2])
    v_copy = pltpu.make_async_copy(v_hbm, values, in_sem.at[3])
    h_copy.start()
    g_copy.start()

    barrier = pltpu.get_barrier_semaphore()
    for d in range(1, rows * narrow):
        other = lax.rem(n * rows + me + d, rows * narrow)
        row = lax.rem(other, rows)
        pl.semaphore_signal(
            barrier, inc=1,
            device_id={"group": row // wide, "wide": lax.rem(row, wide), "narrow": other // rows},
            device_id_type=MESH,
        )

    @pl.loop(0, depth // PIECE)
    def _(c):
        load(c).start()

    h_copy.wait()
    wide_row = h_in[...].astype(jnp.float32)
    for b in range(blocks):
        hf[b : b + 1, :] = wide_row[:, b * HD : (b + 1) * HD]
    own = hf[...]
    squares = jnp.sum(own * own, axis=0, keepdims=True)
    ssown[...] = squares
    g_copy.wait()

    pl.semaphore_wait(barrier, rows * narrow - 1)

    ss_copies = []
    for d in range(1, narrow):
        copy = pltpu.make_async_remote_copy(
            src_ref=ssown, dst_ref=ssrec.at[d],
            send_sem=ss_s.at[d], recv_sem=ss_r.at[d],
            device_id={"narrow": lax.rem(n + d, narrow)},
            device_id_type=MESH,
        )
        copy.start()
        ss_copies.append(copy)
    for d in range(1, narrow):
        ss_copies[d - 1].wait_recv()
        squares = squares + ssrec[d]
    scale = lax.rsqrt(jnp.sum(squares, axis=-1, keepdims=True) / features + norm_eps)
    hsend[...] = (own * scale * gain[...]).astype(jnp.bfloat16)

    def spread(source, target, part, size, send, recv):
        copies = []
        stride = source.shape[0] // ways
        for d in range(1, rows):
            row = lax.rem(me + d, rows)
            at = pl.multiple_of((row // wide) * stride + part * size, size)
            copy = pltpu.make_async_remote_copy(
                src_ref=source.at[pl.ds(at, size)], dst_ref=target.at[me, pl.ds(part * size, size)],
                send_sem=send.at[part, d], recv_sem=recv.at[part, me],
                device_id={"group": row // wide, "wide": lax.rem(row, wide)},
                device_id_type=MESH,
            )
            copy.start()
            copies.append(copy)
        at = pl.multiple_of(y * stride + part * size, size)
        target[me, part * size : (part + 1) * size, :] = source[pl.ds(at, size), :]
        return copies

    def arrive(buffer, part, size, s, recv):
        block = buffer.at[s, pl.ds(part * size, size)]

        @pl.when(s != me)
        def _():
            pltpu.make_async_copy(block, block, recv.at[part, s]).wait()

    half = blocks // ways // PARTS
    h_copies = []
    for part in range(PARTS):
        h_copies += spread(hsend, hrec, part, half, h_s, h_r)

    k_copy.start()
    v_copy.start()

    @pl.loop(0, out_depth // PIECE)
    def _(c):
        load_out(c).start()

    position = len_ref[0].astype(jnp.float32)
    lane = lax.broadcasted_iota(jnp.int32, (1, HD), 1)
    turn = lax.rem(lane, HD // 2).astype(jnp.float32)
    angles = position * jnp.exp(turn * (-2.0 / HD * math.log(rope_theta)))
    cosine = jnp.cos(angles)
    sine = jnp.where(lane < HD // 2, -jnp.sin(angles), jnp.sin(angles))

    deep = half * HD
    total = None
    for part in range(PARTS):
        for s in range(rows):
            arrive(hrec, part, half, s, h_r)
            xs[s * half : (s + 1) * half, :] = hrec[
                s, part * half : (part + 1) * half, :
            ].astype(jnp.float32)
        for b in range(half):
            lhs[:, b * HD : (b + 1) * HD] = xs[pl.ds(b, rows, stride=half), :].astype(jnp.bfloat16)
        for i in range(deep // PIECE):
            load(part * (deep // PIECE) + i).wait()
        product = jnp.dot(
            lhs[...], wq[part * deep : (part + 1) * deep, :], preferred_element_type=jnp.float32
        )
        total = product if total is None else total + product
    for j in range(heads):
        psend[:, j, :] = total[:, j * HD : (j + 1) * HD]

    terms = narrow * ways
    slot = lax.rem(w, share) * terms + n * ways + y
    owner = w // share

    def collect(source, target, send, recv):
        copies = []
        for d in range(rows):
            row = lax.rem(me + d, rows)
            copy = pltpu.make_async_remote_copy(
                src_ref=source.at[row], dst_ref=target.at[slot],
                send_sem=send.at[d], recv_sem=recv.at[slot],
                device_id={"group": row // wide, "wide": lax.rem(row, wide), "narrow": owner},
                device_id_type=MESH,
            )
            if d == 0:
                @pl.when(owner == n)
                def _():
                    pltpu.make_async_copy(source.at[me], target.at[slot], recv.at[slot]).start()

                @pl.when(owner != n)
                def _():
                    copy.start()
            else:
                copy.start()
            copies.append(copy)
        return copies

    def receive(target, recv):
        for s in range(rows):
            pltpu.make_async_copy(target.at[s], target.at[s], recv.at[s]).wait()

    def added(target, b):
        block = target[b * terms]
        for i in range(1, terms):
            block = block + target[b * terms + i]
        return block

    p_copies = collect(psend, prec, p_s, p_r)
    k_copy.wait()
    v_copy.wait()
    receive(prec, p_r)

    per_group = share // groups
    context = keys.shape[1]
    queries = per_group * heads - 2
    for g in range(groups):
        for b in range(per_group):
            joined[g, b * heads : (b + 1) * heads, :] = added(prec, g * per_group + b)
    for g in range(groups):
        turned = joined[g, 0 : queries, :]
        turned = turned * cosine + pltpu.roll(turned, HD // 2, 1) * sine
        query = (turned * HD ** (-0.5)).astype(jnp.bfloat16)
        new_key = joined[g, queries : queries + 1, :]
        new_key = new_key * cosine + pltpu.roll(new_key, HD // 2, 1) * sine
        new_key = new_key.astype(jnp.bfloat16).astype(jnp.float32)
        new_value = joined[g, queries + 1 : queries + 2, :].astype(jnp.bfloat16).astype(jnp.float32)
        scores = lax.dot_general(
            query, keys[0, :, g * HD : (g + 1) * HD], (((1,), (1,)), ((), ())),
            preferred_element_type=jnp.float32,
        )
        own_score = jnp.sum(query.astype(jnp.float32) * new_key, axis=-1, keepdims=True)
        live = lax.broadcasted_iota(jnp.int32, (queries, context), 1) < len_ref[0]
        scores = jnp.where(live, scores, -1e30)
        top = jnp.maximum(jnp.max(scores, axis=-1, keepdims=True), own_score)
        expo = jnp.exp(scores - top)
        own_expo = jnp.exp(own_score - top)
        weight = jnp.sum(expo, axis=-1, keepdims=True) + own_expo
        probs = (expo / weight).astype(jnp.bfloat16)
        mixed = jnp.dot(
            probs, values[0, :, g * HD : (g + 1) * HD], preferred_element_type=jnp.float32
        )
        mixed = mixed + (own_expo / weight) * new_value
        msend[g * queries : (g + 1) * queries, :] = mixed.astype(jnp.bfloat16)

    size = msend.shape[0] // ways
    m_copies = spread(msend, mrec, 0, size, m_s, m_r)
    for s in range(rows):
        arrive(mrec, 0, size, s, m_r)
        ms[s * size : (s + 1) * size, :] = mrec[s].astype(jnp.float32)
    for b in range(size):
        lhs2[:, b * HD : (b + 1) * HD] = ms[pl.ds(b, rows, stride=size), :].astype(jnp.bfloat16)
    for c in range(out_depth // PIECE):
        load_out(c).wait()

    columns = wo.shape[1]
    width = columns // PARTS
    count = width // HD
    o_copies = []
    for part in range(PARTS):
        product = jnp.dot(
            lhs2[...], wo[:, part * width : (part + 1) * width], preferred_element_type=jnp.float32
        )
        for j in range(count):
            osend[part, :, j, :] = product[:, j * HD : (j + 1) * HD]
        o_copies.append(collect(osend.at[part], orec.at[part], o_s.at[part], o_r.at[part]))

    for part in range(PARTS):
        receive(orec.at[part], o_r.at[part])
        for b in range(share):
            start = b * (columns // HD) + part * count
            out_ref[start : start + count, :] = hf[start : start + count, :] + added(orec.at[part], b)

    for copy in ss_copies + h_copies + m_copies:
        copy.wait_send()
    for copies in [p_copies] + o_copies:
        for copy in copies[1:]:
            copy.wait_send()

        @pl.when(owner != n)
        def _():
            copies[0].wait_send()


def fused(sizes, hidden_in, norm_gain, qkv_weight, out_weight, cache_keys, cache_values, cache_lengths):
    ways, wide, narrow = sizes
    depth, columns = qkv_weight.shape
    out_depth, out_columns = out_weight.shape
    heads = columns // HD
    groups = cache_keys.shape[2] // HD
    blocks = depth // HD
    out_blocks = out_columns // HD
    share = wide // narrow
    rows = ways * wide
    part_blocks = blocks // ways // PARTS
    mixed_blocks = out_depth // HD // ways
    bf16, f32 = jnp.bfloat16, jnp.float32
    dma = pltpu.SemaphoreType.DMA
    anywhere = pl.BlockSpec(memory_space=pltpu.HBM)
    out = pl.pallas_call(
        functools.partial(decode_kernel, ways, wide, narrow, heads, groups, depth * narrow),
        out_shape=jax.ShapeDtypeStruct((blocks, HD), f32),
        in_specs=[
            anywhere, anywhere, pl.BlockSpec(memory_space=pltpu.SMEM),
            anywhere, anywhere, anywhere, anywhere,
        ],
        out_specs=pl.BlockSpec(memory_space=pltpu.VMEM),
        scratch_shapes=[
            pltpu.VMEM(hidden_in.shape, bf16),
            pltpu.VMEM((blocks, HD), f32),
            pltpu.VMEM(cache_keys.shape, bf16),
            pltpu.VMEM(cache_values.shape, bf16),
            pltpu.VMEM((depth // ways, columns), bf16),
            pltpu.VMEM((out_depth // ways, out_columns), bf16),
            pltpu.VMEM((blocks, HD), f32),
            pltpu.VMEM((blocks, HD), bf16),
            pltpu.VMEM((rows, blocks // ways, HD), bf16),
            pltpu.VMEM((rows * part_blocks, HD), f32),
            pltpu.VMEM((rows, part_blocks * HD), bf16),
            pltpu.VMEM((1, HD), f32),
            pltpu.VMEM((narrow, 1, HD), f32),
            pltpu.VMEM((rows, heads, HD), f32),
            pltpu.VMEM((rows, heads, HD), f32),
            pltpu.VMEM((groups, share // groups * heads, HD), f32),
            pltpu.VMEM((out_depth // HD, HD), bf16),
            pltpu.VMEM((rows, mixed_blocks, HD), bf16),
            pltpu.VMEM((rows * mixed_blocks, HD), f32),
            pltpu.VMEM((rows, mixed_blocks * HD), bf16),
            pltpu.VMEM((PARTS, rows, out_blocks // PARTS, HD), f32),
            pltpu.VMEM((PARTS, rows, out_blocks // PARTS, HD), f32),
            dma((4,)), dma((depth // ways // PIECE,)), dma((out_depth // ways // PIECE,)),
            dma((narrow,)), dma((narrow,)),
            dma((PARTS, rows)), dma((PARTS, rows)),
            dma((rows,)), dma((rows,)),
            dma((1, rows)), dma((1, rows)),
            dma((PARTS, rows)), dma((PARTS, rows)),
        ],
        compiler_params=pltpu.CompilerParams(
            collective_id=0, has_side_effects=True,
            vmem_limit_bytes=63 * 1024 * 1024 + 768 * 1024,
        ),
        cost_estimate=pl.CostEstimate(
            flops=2 * wide * (depth * columns + out_depth * out_columns),
            bytes_accessed=2 * (depth * columns + out_depth * out_columns) // ways,
            transcendentals=0,
        ),
        name="decode",
    )(
        hidden_in, norm_gain.reshape(blocks, HD), cache_lengths,
        cache_keys, cache_values, qkv_weight, out_weight,
    )
    return out.reshape(1, blocks * HD)


def fits(sizes, hidden_in, qkv_weight, out_weight, cache_keys):
    ways, wide, narrow = sizes
    columns = qkv_weight.shape[1]
    groups = cache_keys.shape[2] // HD
    if hidden_in.shape[0] != 1 or columns % HD or out_weight.shape[1] % (PARTS * 8 * HD):
        return False
    if wide % narrow or (wide // narrow) % groups or ways * wide % 16:
        return False
    if qkv_weight.shape[0] % (ways * PARTS * STEP) or out_weight.shape[0] % (ways * STEP):
        return False
    queries = (wide // narrow) // groups * (columns // HD) - 2
    return queries % 16 == 0 and queries * groups * HD == out_weight.shape[0]


def rotary(values, position):
    half = values.shape[-1] // 2
    frequency = rope_theta ** (-jnp.arange(half, dtype=jnp.float32) * 2.0 / values.shape[-1])
    angles = position[..., None] * frequency
    cosine = jnp.cos(angles)
    sine = jnp.sin(angles)
    first = values[..., :half]
    second = values[..., half:]
    return jnp.concatenate([first * cosine - second * sine, second * cosine + first * sine], -1)


def attend(joined, keys, values, lengths):
    count = joined.shape[0]
    groups = joined.shape[1]
    share = joined.shape[2] - 2
    head_dim = joined.shape[3]
    capacity = keys.shape[1]
    position = lengths.astype(jnp.float32)
    query = (rotary(joined[:, :, :share], position[:, None, None]) * head_dim ** (-0.5)).astype(
        jnp.bfloat16
    )
    new_key = rotary(joined[:, :, share], position[:, None]).astype(jnp.bfloat16)
    new_value = joined[:, :, share + 1].astype(jnp.bfloat16)
    keys_four = keys.reshape(count, capacity, groups, head_dim)
    values_four = values.reshape(count, capacity, groups, head_dim)
    scores = jnp.einsum("bgjd,btgd->bgjt", query, keys_four, preferred_element_type=jnp.float32)
    own = jnp.sum(query.astype(jnp.float32) * new_key.astype(jnp.float32)[:, :, None, :], -1)
    live = jnp.arange(capacity)[None, None, None, :] < lengths[:, None, None, None]
    scores = jnp.where(live, scores, -1e30)
    top = jnp.maximum(jnp.max(scores, -1), own)
    expo = jnp.exp(scores - top[..., None])
    own_expo = jnp.exp(own - top)
    total = jnp.sum(expo, -1) + own_expo
    probs = (expo / total[..., None]).astype(jnp.bfloat16)
    mixed = jnp.einsum("bgjt,btgd->bgjd", probs, values_four, preferred_element_type=jnp.float32)
    mixed = mixed + (own_expo / total)[..., None] * new_value.astype(jnp.float32)[:, :, None, :]
    return mixed.astype(jnp.bfloat16).reshape(count, groups * share * head_dim)


def body(hidden_in, norm_gain, qkv_weight, out_weight, cache_keys, cache_values, cache_lengths):
    sizes = [lax.axis_size(name) for name in ("group", "wide", "narrow")]
    if fits(sizes, hidden_in, qkv_weight, out_weight, cache_keys):
        return fused(
            sizes, hidden_in, norm_gain, qkv_weight, out_weight,
            cache_keys, cache_values, cache_lengths,
        )
    inputs = hidden_in.astype(jnp.float32)
    row_count = hidden_in.shape[0]
    squares = lax.psum(jnp.sum(inputs * inputs, -1), "narrow")
    normed = (inputs * lax.rsqrt(squares / (hidden_in.shape[1] * sizes[2]) + norm_eps)[:, None] * norm_gain).astype(jnp.bfloat16)
    partial_qkv = jnp.dot(
        lax.all_gather(normed, "wide", axis=0, tiled=True),
        qkv_weight,
        preferred_element_type=jnp.float32,
    )
    all_rows, col_block = partial_qkv.shape
    halves = partial_qkv.reshape(all_rows, 1, 2, col_block // 2)
    paired = lax.psum_scatter(halves, "narrow", scatter_dimension=2, tiled=True)
    moved = lax.all_to_all(paired, "wide", split_axis=0, concat_axis=1, tiled=True)
    blocks = moved.shape[1]
    parted = moved.reshape(row_count, 2, blocks // 2, 1, col_block // 2)
    owned = lax.all_to_all(parted, "narrow", split_axis=1, concat_axis=3, tiled=True)
    owned = owned.reshape(row_count, blocks // 2 * col_block)
    groups = cache_keys.shape[2] // HD
    owned = owned.reshape(row_count, groups, owned.shape[1] // (groups * HD), HD)
    mixed = attend(owned, cache_keys, cache_values, cache_lengths)
    partial_out = jnp.dot(
        lax.all_gather(mixed, "wide", axis=0, tiled=True),
        out_weight,
        preferred_element_type=jnp.float32,
    )
    all_rows, col_block = partial_out.shape
    halves = partial_out.reshape(all_rows, 1, 2, col_block // 2)
    paired = lax.psum_scatter(halves, "narrow", scatter_dimension=2, tiled=True)
    moved = lax.all_to_all(paired, "wide", split_axis=0, concat_axis=1, tiled=True)
    blocks = moved.shape[1]
    parted = moved.reshape(row_count, 2, blocks // 2, 1, col_block // 2)
    added = lax.all_to_all(parted, "narrow", split_axis=1, concat_axis=3, tiled=True)
    added = added.reshape(row_count, blocks // 2 * col_block)
    return inputs + added


def solution(mesh):
    placed = (
        P(("group", "wide"), "narrow"),
        P("narrow"),
        P("narrow", "wide"),
        P("narrow", "wide"),
        P(("group", "wide"), None, "narrow"),
        P(("group", "wide"), None, "narrow"),
        P(("group", "wide")),
    )
    return jax.shard_map(
        body, mesh=mesh, in_specs=placed, out_specs=P(("group", "wide"), "narrow"), check_vma=False
    )
```

```python
import functools
import math

import jax
import jax.numpy as jnp
from jax import lax
from jax.experimental import pallas as pl
from jax.experimental.pallas import tpu as pltpu
from jax.sharding import PartitionSpec as P

HD = 128


rope_theta = 500000.0
norm_eps = 1e-05
MESH = pl.DeviceIdType.MESH


PIECE = 1024
STEP = 2048


def decode_kernel(
    wide, narrow, heads, groups, features,
    h_hbm, g_hbm, len_ref, k_hbm, v_hbm, wq_hbm, wo_hbm, out_ref,
    h_in, gain, keys, values, wq, wo, hf, hsend, hrec, xs, lhs, ssown, ssrec, psend, prec, joined,
    msend, mrec, ms, lhs2, osend, orec,
    in_sem, q_sem, w_sem, ss_s, ss_r, h_s, h_r, p_s, p_r, m_s, m_r, o_s, o_r,
):
    w = lax.axis_index("wide")
    n = lax.axis_index("narrow")
    share = wide // narrow
    blocks = hf.shape[0]
    depth, out_depth = wq.shape[0], wo.shape[0]
    turns = [w] + [lax.rem(w + d, wide) for d in range(1, wide)]

    def load(weights, held, sem, step):
        for i in range(STEP // PIECE):
            at = pl.ds(step * STEP + i * PIECE, PIECE)
            pltpu.make_async_copy(weights.at[at, :], held.at[at, :], sem.at[step]).start()

    def loaded(held, sem, step):
        block = held.at[pl.ds(step * STEP, STEP), :]
        pltpu.make_async_copy(block, block, sem.at[step]).wait()

    h_copy = pltpu.make_async_copy(h_hbm, h_in, in_sem.at[0])
    g_copy = pltpu.make_async_copy(g_hbm, gain, in_sem.at[1])
    k_copy = pltpu.make_async_copy(k_hbm, keys, in_sem.at[2])
    v_copy = pltpu.make_async_copy(v_hbm, values, in_sem.at[3])
    h_copy.start()
    g_copy.start()

    barrier = pltpu.get_barrier_semaphore()
    for d in range(wide):
        for e in range(narrow):
            if d or e:
                pl.semaphore_signal(
                    barrier, inc=1,
                    device_id={"wide": turns[d], "narrow": lax.rem(n + e, narrow)},
                    device_id_type=MESH,
                )

    for step in range(depth // STEP):
        load(wq_hbm, wq, q_sem, step)

    h_copy.wait()
    wide_row = h_in[...].astype(jnp.float32)
    for b in range(blocks):
        hf[b : b + 1, :] = wide_row[:, b * HD : (b + 1) * HD]
    own = hf[...]
    squares = jnp.sum(own * own, axis=0, keepdims=True)
    ssown[...] = squares
    g_copy.wait()

    pl.semaphore_wait(barrier, wide * narrow - 1)

    ss_copies = []
    for d in range(1, narrow):
        copy = pltpu.make_async_remote_copy(
            src_ref=ssown, dst_ref=ssrec.at[d],
            send_sem=ss_s.at[d], recv_sem=ss_r.at[d],
            device_id={"narrow": lax.rem(n + d, narrow)},
            device_id_type=MESH,
        )
        copy.start()
        ss_copies.append(copy)
    for d in range(1, narrow):
        ss_copies[d - 1].wait_recv()
        squares = squares + ssrec[d]
    scale = lax.rsqrt(jnp.sum(squares, axis=-1, keepdims=True) / features + norm_eps)
    hsend[...] = (own * scale * gain[...]).astype(jnp.bfloat16)

    def spread(source, target, send, recv):
        for d in range(1, wide):
            pltpu.make_async_remote_copy(
                src_ref=source, dst_ref=target.at[w],
                send_sem=send.at[0], recv_sem=recv.at[0],
                device_id={"wide": turns[d]},
                device_id_type=MESH,
            ).start()
        target[w] = source[...]

    def wait_for(buffer, count, sem):
        block = buffer.at[pl.ds(0, count)]
        pltpu.make_async_copy(block, block, sem.at[0]).wait()

    spread(hsend, hrec, h_s, h_r)
    k_copy.start()
    v_copy.start()
    for step in range(out_depth // STEP):
        load(wo_hbm, wo, w_sem, step)

    position = len_ref[0].astype(jnp.float32)
    lane = lax.broadcasted_iota(jnp.int32, (1, HD), 1)
    turn = lax.rem(lane, HD // 2).astype(jnp.float32)
    angles = position * jnp.exp(turn * (-2.0 / HD * math.log(rope_theta)))
    cosine = jnp.cos(angles)
    sine = jnp.where(lane < HD // 2, -jnp.sin(angles), jnp.sin(angles))

    def multiply(rows_in, flat, left, held, sem):
        count = rows_in.shape[1]
        for s in range(wide):
            flat[s * count : (s + 1) * count, :] = rows_in[s].astype(jnp.float32)
        per = STEP // HD
        total = None
        for step in range(count // per):
            for b in range(step * per, (step + 1) * per):
                left[:, b * HD : (b + 1) * HD] = flat[
                    pl.ds(b, wide, stride=count), :
                ].astype(jnp.bfloat16)
            loaded(held, sem, step)
            at = slice(step * STEP, (step + 1) * STEP)
            product = jnp.dot(left[:, at], held[at, :], preferred_element_type=jnp.float32)
            total = product if total is None else total + product
        return total

    wait_for(hrec, wide - 1, h_r)
    total = multiply(hrec, xs, lhs, wq, q_sem)
    for j in range(heads):
        psend[:, j, :] = total[:, j * HD : (j + 1) * HD]

    slot = lax.rem(w, share) * narrow + n
    owner = w // share

    def collect(source, target, send, recv):
        for d in range(wide):
            copy = pltpu.make_async_remote_copy(
                src_ref=source.at[turns[d]], dst_ref=target.at[slot],
                send_sem=send.at[0], recv_sem=recv.at[0],
                device_id={"wide": turns[d], "narrow": owner},
                device_id_type=MESH,
            )
            if d:
                copy.start()
                continue

            @pl.when(owner == n)
            def _():
                pltpu.make_async_copy(source.at[w], target.at[slot], recv.at[0]).start()

            @pl.when(owner != n)
            def _():
                copy.start()

    def added(target, b):
        block = target[b * narrow]
        for i in range(1, narrow):
            block = block + target[b * narrow + i]
        return block

    collect(psend, prec, p_s, p_r)
    k_copy.wait()
    v_copy.wait()
    wait_for(prec, wide, p_r)

    per_group = share // groups
    context = keys.shape[1]
    queries = per_group * heads - 2
    for g in range(groups):
        for b in range(per_group):
            joined[g, b * heads : (b + 1) * heads, :] = added(prec, g * per_group + b)
    for g in range(groups):
        turned = joined[g, 0 : queries, :]
        turned = turned * cosine + pltpu.roll(turned, HD // 2, 1) * sine
        query = (turned * HD ** (-0.5)).astype(jnp.bfloat16)
        new_key = joined[g, queries : queries + 1, :]
        new_key = new_key * cosine + pltpu.roll(new_key, HD // 2, 1) * sine
        new_key = new_key.astype(jnp.bfloat16).astype(jnp.float32)
        new_value = joined[g, queries + 1 : queries + 2, :].astype(jnp.bfloat16).astype(jnp.float32)
        scores = lax.dot_general(
            query, keys[0, :, g * HD : (g + 1) * HD], (((1,), (1,)), ((), ())),
            preferred_element_type=jnp.float32,
        )
        own_score = jnp.sum(query.astype(jnp.float32) * new_key, axis=-1, keepdims=True)
        live = lax.broadcasted_iota(jnp.int32, (queries, context), 1) < len_ref[0]
        scores = jnp.where(live, scores, -1e30)
        top = jnp.maximum(jnp.max(scores, axis=-1, keepdims=True), own_score)
        expo = jnp.exp(scores - top)
        own_expo = jnp.exp(own_score - top)
        weight = jnp.sum(expo, axis=-1, keepdims=True) + own_expo
        probs = (expo / weight).astype(jnp.bfloat16)
        mixed = jnp.dot(
            probs, values[0, :, g * HD : (g + 1) * HD], preferred_element_type=jnp.float32
        )
        mixed = mixed + (own_expo / weight) * new_value
        msend[g * queries : (g + 1) * queries, :] = mixed.astype(jnp.bfloat16)

    spread(msend, mrec, m_s, m_r)
    wait_for(mrec, wide - 1, m_r)
    total = multiply(mrec, ms, lhs2, wo, w_sem)
    count = wo.shape[1] // HD
    for j in range(count):
        osend[:, j, :] = total[:, j * HD : (j + 1) * HD]
    collect(osend, orec, o_s, o_r)
    wait_for(orec, wide, o_r)
    for b in range(share):
        out_ref[b * count : (b + 1) * count, :] = added(orec, b)

    for copy in ss_copies:
        copy.wait_send()
    wait_for(hrec, wide - 1, h_s)
    wait_for(prec, wide - 1, p_s)
    wait_for(mrec, wide - 1, m_s)
    wait_for(orec, wide - 1, o_s)

    @pl.when(owner != n)
    def _():
        wait_for(prec, 1, p_s)
        wait_for(orec, 1, o_s)


def fused(sizes, hidden_in, norm_gain, qkv_weight, out_weight, cache_keys, cache_values, cache_lengths):
    wide, narrow = sizes
    depth, columns = qkv_weight.shape
    out_depth, out_columns = out_weight.shape
    heads = columns // HD
    groups = cache_keys.shape[2] // HD
    blocks = depth // HD
    out_blocks = out_columns // HD
    share = wide // narrow
    mixed_blocks = out_depth // HD
    bf16, f32 = jnp.bfloat16, jnp.float32
    dma = pltpu.SemaphoreType.DMA
    anywhere = pl.BlockSpec(memory_space=pltpu.HBM)
    out = pl.pallas_call(
        functools.partial(decode_kernel, wide, narrow, heads, groups, depth * narrow),
        out_shape=jax.ShapeDtypeStruct((blocks, HD), f32),
        in_specs=[
            anywhere, anywhere, pl.BlockSpec(memory_space=pltpu.SMEM),
            anywhere, anywhere, anywhere, anywhere,
        ],
        out_specs=pl.BlockSpec(memory_space=pltpu.VMEM),
        scratch_shapes=[
            pltpu.VMEM(hidden_in.shape, bf16),
            pltpu.VMEM((blocks, HD), f32),
            pltpu.VMEM(cache_keys.shape, bf16),
            pltpu.VMEM(cache_values.shape, bf16),
            pltpu.VMEM((depth, columns), bf16),
            pltpu.VMEM((out_depth, out_columns), bf16),
            pltpu.VMEM((blocks, HD), f32),
            pltpu.VMEM((blocks, HD), bf16),
            pltpu.VMEM((wide, blocks, HD), bf16),
            pltpu.VMEM((wide * blocks, HD), f32),
            pltpu.VMEM((wide, depth), bf16),
            pltpu.VMEM((1, HD), f32),
            pltpu.VMEM((narrow, 1, HD), f32),
            pltpu.VMEM((wide, heads, HD), f32),
            pltpu.VMEM((wide, heads, HD), f32),
            pltpu.VMEM((groups, share // groups * heads, HD), f32),
            pltpu.VMEM((mixed_blocks, HD), bf16),
            pltpu.VMEM((wide, mixed_blocks, HD), bf16),
            pltpu.VMEM((wide * mixed_blocks, HD), f32),
            pltpu.VMEM((wide, out_depth), bf16),
            pltpu.VMEM((wide, out_blocks, HD), f32),
            pltpu.VMEM((wide, out_blocks, HD), f32),
            dma((4,)), dma((depth // STEP,)), dma((out_depth // STEP,)),
            dma((narrow,)), dma((narrow,)),
            dma((1,)), dma((1,)),
            dma((1,)), dma((1,)),
            dma((1,)), dma((1,)),
            dma((1,)), dma((1,)),
        ],
        compiler_params=pltpu.CompilerParams(
            collective_id=0, has_side_effects=True,
            vmem_limit_bytes=63 * 1024 * 1024 + 768 * 1024,
        ),
        cost_estimate=pl.CostEstimate(
            flops=2 * wide * (depth * columns + out_depth * out_columns),
            bytes_accessed=2 * (depth * columns + out_depth * out_columns),
            transcendentals=0,
        ),
        name="decode",
    )(
        hidden_in, norm_gain.reshape(blocks, HD), cache_lengths,
        cache_keys, cache_values, qkv_weight, out_weight,
    )
    return hidden_in.astype(f32) + out.reshape(1, blocks * HD)


def fits(sizes, hidden_in, qkv_weight, out_weight, cache_keys):
    wide, narrow = sizes
    columns = qkv_weight.shape[1]
    groups = cache_keys.shape[2] // HD
    if hidden_in.shape[0] != 1 or columns % HD or out_weight.shape[1] % (8 * HD):
        return False
    if wide % narrow or (wide // narrow) % groups or wide % 8:
        return False
    if qkv_weight.shape[0] % STEP or out_weight.shape[0] % STEP:
        return False
    queries = (wide // narrow) // groups * (columns // HD) - 2
    return queries % 16 == 0 and queries * groups * HD == out_weight.shape[0]


def rotary(values, position):
    half = values.shape[-1] // 2
    frequency = rope_theta ** (-jnp.arange(half, dtype=jnp.float32) * 2.0 / values.shape[-1])
    angles = position[..., None] * frequency
    cosine = jnp.cos(angles)
    sine = jnp.sin(angles)
    first = values[..., :half]
    second = values[..., half:]
    return jnp.concatenate([first * cosine - second * sine, second * cosine + first * sine], -1)


def attend(joined, keys, values, lengths):
    count = joined.shape[0]
    groups = joined.shape[1]
    share = joined.shape[2] - 2
    head_dim = joined.shape[3]
    capacity = keys.shape[1]
    position = lengths.astype(jnp.float32)
    query = (rotary(joined[:, :, :share], position[:, None, None]) * head_dim ** (-0.5)).astype(
        jnp.bfloat16
    )
    new_key = rotary(joined[:, :, share], position[:, None]).astype(jnp.bfloat16)
    new_value = joined[:, :, share + 1].astype(jnp.bfloat16)
    keys_four = keys.reshape(count, capacity, groups, head_dim)
    values_four = values.reshape(count, capacity, groups, head_dim)
    scores = jnp.einsum("bgjd,btgd->bgjt", query, keys_four, preferred_element_type=jnp.float32)
    own = jnp.sum(query.astype(jnp.float32) * new_key.astype(jnp.float32)[:, :, None, :], -1)
    live = jnp.arange(capacity)[None, None, None, :] < lengths[:, None, None, None]
    scores = jnp.where(live, scores, -1e30)
    top = jnp.maximum(jnp.max(scores, -1), own)
    expo = jnp.exp(scores - top[..., None])
    own_expo = jnp.exp(own - top)
    total = jnp.sum(expo, -1) + own_expo
    probs = (expo / total[..., None]).astype(jnp.bfloat16)
    mixed = jnp.einsum("bgjt,btgd->bgjd", probs, values_four, preferred_element_type=jnp.float32)
    mixed = mixed + (own_expo / total)[..., None] * new_value.astype(jnp.float32)[:, :, None, :]
    return mixed.astype(jnp.bfloat16).reshape(count, groups * share * head_dim)


def body(hidden_in, norm_gain, qkv_weight, out_weight, cache_keys, cache_values, cache_lengths):
    sizes = [lax.axis_size(name) for name in ("wide", "narrow")]
    if fits(sizes, hidden_in, qkv_weight, out_weight, cache_keys):
        return fused(
            sizes, hidden_in, norm_gain, qkv_weight, out_weight,
            cache_keys, cache_values, cache_lengths,
        )
    inputs = hidden_in.astype(jnp.float32)
    row_count = hidden_in.shape[0]
    squares = lax.psum(jnp.sum(inputs * inputs, -1), "narrow")
    normed = (inputs * lax.rsqrt(squares / (hidden_in.shape[1] * sizes[1]) + norm_eps)[:, None] * norm_gain).astype(jnp.bfloat16)
    partial_qkv = jnp.dot(
        lax.all_gather(normed, "wide", axis=0, tiled=True),
        qkv_weight,
        preferred_element_type=jnp.float32,
    )
    all_rows, col_block = partial_qkv.shape
    halves = partial_qkv.reshape(all_rows, 1, 2, col_block // 2)
    paired = lax.psum_scatter(halves, "narrow", scatter_dimension=2, tiled=True)
    moved = lax.all_to_all(paired, "wide", split_axis=0, concat_axis=1, tiled=True)
    blocks = moved.shape[1]
    parted = moved.reshape(row_count, 2, blocks // 2, 1, col_block // 2)
    owned = lax.all_to_all(parted, "narrow", split_axis=1, concat_axis=3, tiled=True)
    owned = owned.reshape(row_count, blocks // 2 * col_block)
    groups = cache_keys.shape[2] // HD
    owned = owned.reshape(row_count, groups, owned.shape[1] // (groups * HD), HD)
    mixed = attend(owned, cache_keys, cache_values, cache_lengths)
    partial_out = jnp.dot(
        lax.all_gather(mixed, "wide", axis=0, tiled=True),
        out_weight,
        preferred_element_type=jnp.float32,
    )
    all_rows, col_block = partial_out.shape
    halves = partial_out.reshape(all_rows, 1, 2, col_block // 2)
    paired = lax.psum_scatter(halves, "narrow", scatter_dimension=2, tiled=True)
    moved = lax.all_to_all(paired, "wide", split_axis=0, concat_axis=1, tiled=True)
    blocks = moved.shape[1]
    parted = moved.reshape(row_count, 2, blocks // 2, 1, col_block // 2)
    added = lax.all_to_all(parted, "narrow", split_axis=1, concat_axis=3, tiled=True)
    added = added.reshape(row_count, blocks // 2 * col_block)
    return inputs + added


def solution(mesh):
    placed = (
        P(("group", "wide"), "narrow"),
        P("narrow"),
        P("narrow", "wide"),
        P("narrow", "wide"),
        P(("group", "wide"), None, "narrow"),
        P(("group", "wide"), None, "narrow"),
        P(("group", "wide")),
    )
    return jax.shard_map(
        body, mesh=mesh, in_specs=placed, out_specs=P(("group", "wide"), "narrow"), check_vma=False
    )
```

```python
import functools
import math

import jax
import jax.numpy as jnp
from jax import lax
from jax.experimental import pallas as pl
from jax.experimental.pallas import tpu as pltpu
from jax.sharding import PartitionSpec as P

HD = 128


rope_theta = 500000.0
norm_eps = 1e-05
MESH = pl.DeviceIdType.MESH


PARTS = 2
PIECE = 1024
STEP = 2048


def decode_kernel(
    wide, narrow, heads, groups, features,
    h_hbm, g_hbm, len_ref, k_hbm, v_hbm, wq_hbm, wo_hbm, out_ref,
    h_in, gain, keys, values, wq, wo, hf, hsend, hrec, xs, lhs, ssrec, psend, prec, joined,
    msend, mrec, ms, lhs2, osend, orec,
    in_sem, q_sem, w_sem, ss_s, ss_r, h_s, h_r, p_s, p_r, m_s, m_r, o_s, o_r,
):
    w = lax.axis_index("wide")
    n = lax.axis_index("narrow")
    share = wide // narrow
    blocks = hf.shape[0]
    depth, out_depth = wq.shape[0], wo.shape[0]
    turns = [w] + [lax.rem(w + d, wide) for d in range(1, wide)]

    def load(weights, held, sem, step):
        for i in range(STEP // PIECE):
            at = pl.ds(step * STEP + i * PIECE, PIECE)
            pltpu.make_async_copy(weights.at[at, :], held.at[at, :], sem.at[step]).start()

    def loaded(held, sem, step):
        block = held.at[pl.ds(step * STEP, STEP), :]
        pltpu.make_async_copy(block, block, sem.at[step]).wait()

    h_copy = pltpu.make_async_copy(h_hbm, h_in, in_sem.at[0])
    g_copy = pltpu.make_async_copy(g_hbm, gain, in_sem.at[1])
    k_copy = pltpu.make_async_copy(k_hbm, keys, in_sem.at[2])
    v_copy = pltpu.make_async_copy(v_hbm, values, in_sem.at[3])
    h_copy.start()
    g_copy.start()

    barrier = pltpu.get_barrier_semaphore()
    for d in range(wide):
        for e in range(narrow):
            if d or e:
                pl.semaphore_signal(
                    barrier, inc=1,
                    device_id={"wide": turns[d], "narrow": lax.rem(n + e, narrow)},
                    device_id_type=MESH,
                )

    for step in range(depth // STEP):
        load(wq_hbm, wq, q_sem, step)

    h_copy.wait()
    wide_row = h_in[...].astype(jnp.float32)
    for b in range(blocks):
        hf[b : b + 1, :] = wide_row[:, b * HD : (b + 1) * HD]
    own = hf[...]
    squares = jnp.sum(own * own, axis=0, keepdims=True)
    me = n * wide + w
    ssrec[me] = squares
    hsend[...] = own.astype(jnp.bfloat16)
    g_copy.wait()

    pl.semaphore_wait(barrier, wide * narrow - 1)

    def spread(source, target, part, send, recv):
        size = target.shape[2]
        block = source.at[pl.ds(part * size, size)]
        for d in range(1, wide):
            pltpu.make_async_remote_copy(
                src_ref=block, dst_ref=target.at[part, w],
                send_sem=send.at[part], recv_sem=recv.at[part],
                device_id={"wide": turns[d]},
                device_id_type=MESH,
            ).start()
        target[part, w] = block[...]

    def wait_for(buffer, count, sem):
        block = buffer.at[pl.ds(0, count)]
        pltpu.make_async_copy(block, block, sem).wait()

    for d in range(wide):
        for e in range(narrow):
            if d or e:
                pltpu.make_async_remote_copy(
                    src_ref=ssrec.at[me], dst_ref=ssrec.at[me],
                    send_sem=ss_s.at[0], recv_sem=ss_r.at[0],
                    device_id={"wide": turns[d], "narrow": lax.rem(n + e, narrow)},
                    device_id_type=MESH,
                ).start()
    for part in range(PARTS):
        spread(hsend, hrec, part, h_s, h_r)
    k_copy.start()
    v_copy.start()
    for step in range(out_depth // STEP):
        load(wo_hbm, wo, w_sem, step)

    position = len_ref[0].astype(jnp.float32)
    lane = lax.broadcasted_iota(jnp.int32, (1, HD), 1)
    turn = lax.rem(lane, HD // 2).astype(jnp.float32)
    angles = position * jnp.exp(turn * (-2.0 / HD * math.log(rope_theta)))
    cosine = jnp.cos(angles)
    sine = jnp.where(lane < HD // 2, -jnp.sin(angles), jnp.sin(angles))

    wait_for(ssrec, wide * narrow - 1, ss_r.at[0])
    squares = ssrec[0:wide]
    for part in range(1, narrow):
        squares = squares + ssrec[part * wide : (part + 1) * wide]
    scale = lax.rsqrt(jnp.sum(squares, axis=-1, keepdims=True) / features + norm_eps)
    per = STEP // HD
    half = blocks // PARTS
    total = None
    for part in range(PARTS):
        wait_for(hrec.at[part], wide - 1, h_r.at[part])
        gains = gain[part * half : (part + 1) * half, :]
        for s in range(wide):
            xs[s * half : (s + 1) * half, :] = hrec[part, s].astype(jnp.float32) * scale[s] * gains
        for step in range(half // per):
            for b in range(per):
                lhs[:, b * HD : (b + 1) * HD] = xs[
                    pl.ds(step * per + b, wide, stride=half), :
                ].astype(jnp.bfloat16)
            at = part * (half // per) + step
            loaded(wq, q_sem, at)
            product = jnp.dot(
                lhs[...], wq[at * STEP : (at + 1) * STEP, :], preferred_element_type=jnp.float32
            )
            total = product if total is None else total + product
    for j in range(heads):
        psend[:, j, :] = total[:, j * HD : (j + 1) * HD]

    slot = lax.rem(w, share) * narrow + n
    owner = w // share

    def collect(source, target, send, recv):
        for d in range(wide):
            copy = pltpu.make_async_remote_copy(
                src_ref=source.at[turns[d]], dst_ref=target.at[slot],
                send_sem=send, recv_sem=recv,
                device_id={"wide": turns[d], "narrow": owner},
                device_id_type=MESH,
            )
            if d:
                copy.start()
                continue

            @pl.when(owner == n)
            def _():
                pltpu.make_async_copy(source.at[w], target.at[slot], recv).start()

            @pl.when(owner != n)
            def _():
                copy.start()

    def added(target, b):
        block = target[b * narrow]
        for i in range(1, narrow):
            block = block + target[b * narrow + i]
        return block

    collect(psend, prec, p_s.at[0], p_r.at[0])
    k_copy.wait()
    v_copy.wait()
    wait_for(prec, wide, p_r.at[0])

    per_group = share // groups
    context = keys.shape[1]
    queries = per_group * heads - 2
    for g in range(groups):
        for b in range(per_group):
            joined[g, b * heads : (b + 1) * heads, :] = added(prec, g * per_group + b)
    for g in range(groups):
        turned = joined[g, 0 : queries, :]
        turned = turned * cosine + pltpu.roll(turned, HD // 2, 1) * sine
        query = (turned * HD ** (-0.5)).astype(jnp.bfloat16)
        new_key = joined[g, queries : queries + 1, :]
        new_key = new_key * cosine + pltpu.roll(new_key, HD // 2, 1) * sine
        new_key = new_key.astype(jnp.bfloat16).astype(jnp.float32)
        new_value = joined[g, queries + 1 : queries + 2, :].astype(jnp.bfloat16).astype(jnp.float32)
        scores = lax.dot_general(
            query, keys[0, :, g * HD : (g + 1) * HD], (((1,), (1,)), ((), ())),
            preferred_element_type=jnp.float32,
        )
        own_score = jnp.sum(query.astype(jnp.float32) * new_key, axis=-1, keepdims=True)
        live = lax.broadcasted_iota(jnp.int32, (queries, context), 1) < len_ref[0]
        scores = jnp.where(live, scores, -1e30)
        top = jnp.maximum(jnp.max(scores, axis=-1, keepdims=True), own_score)
        expo = jnp.exp(scores - top)
        own_expo = jnp.exp(own_score - top)
        weight = jnp.sum(expo, axis=-1, keepdims=True) + own_expo
        probs = (expo / weight).astype(jnp.bfloat16)
        mixed = jnp.dot(
            probs, values[0, :, g * HD : (g + 1) * HD], preferred_element_type=jnp.float32
        )
        mixed = mixed + (own_expo / weight) * new_value
        msend[g * queries : (g + 1) * queries, :] = mixed.astype(jnp.bfloat16)
        spread(msend, mrec, g, m_s, m_r)

    deep = queries * HD
    width = wo.shape[1] // PARTS
    count = width // HD
    total = None
    for g in range(groups):
        wait_for(mrec.at[g], wide - 1, m_r.at[g])
        for s in range(wide):
            ms[s * queries : (s + 1) * queries, :] = mrec[g, s].astype(jnp.float32)
        for b in range(queries):
            lhs2[:, b * HD : (b + 1) * HD] = ms[
                pl.ds(b, wide, stride=queries), :
            ].astype(jnp.bfloat16)
        for step in range(g * deep // STEP, (g + 1) * deep // STEP):
            loaded(wo, w_sem, step)
        if g < groups - 1:
            product = jnp.dot(
                lhs2[...], wo[g * deep : (g + 1) * deep, :], preferred_element_type=jnp.float32
            )
            total = product if total is None else total + product
            continue
        for part in range(PARTS):
            at = slice(part * width, (part + 1) * width)
            product = jnp.dot(
                lhs2[...], wo[g * deep : (g + 1) * deep, at], preferred_element_type=jnp.float32
            )
            if total is not None:
                product = total[:, at] + product
            for j in range(count):
                osend[part, :, j, :] = product[:, j * HD : (j + 1) * HD]
            collect(osend.at[part], orec.at[part], o_s.at[part], o_r.at[part])

    for part in range(PARTS):
        wait_for(orec.at[part], wide, o_r.at[part])
        for b in range(share):
            start = (b * PARTS + part) * count
            out_ref[start : start + count, :] = hf[start : start + count, :] + added(orec.at[part], b)

    wait_for(ssrec, wide * narrow - 1, ss_s.at[0])
    sent = [(hrec.at[part], h_s.at[part]) for part in range(PARTS)]
    sent += [(mrec.at[g], m_s.at[g]) for g in range(groups)]
    shared = [(prec, p_s.at[0])]
    shared += [(orec.at[part], o_s.at[part]) for part in range(PARTS)]
    for buffer, sem in sent + shared:
        wait_for(buffer, wide - 1, sem)

    @pl.when(owner != n)
    def _():
        for buffer, sem in shared:
            wait_for(buffer, 1, sem)


def fused(sizes, hidden_in, norm_gain, qkv_weight, out_weight, cache_keys, cache_values, cache_lengths):
    wide, narrow = sizes
    depth, columns = qkv_weight.shape
    out_depth, out_columns = out_weight.shape
    heads = columns // HD
    groups = cache_keys.shape[2] // HD
    blocks = depth // HD
    out_blocks = out_columns // HD
    share = wide // narrow
    mixed_blocks = out_depth // HD
    bf16, f32 = jnp.bfloat16, jnp.float32
    dma = pltpu.SemaphoreType.DMA
    anywhere = pl.BlockSpec(memory_space=pltpu.HBM)
    out = pl.pallas_call(
        functools.partial(decode_kernel, wide, narrow, heads, groups, depth * narrow),
        out_shape=jax.ShapeDtypeStruct((blocks, HD), f32),
        in_specs=[
            anywhere, anywhere, pl.BlockSpec(memory_space=pltpu.SMEM),
            anywhere, anywhere, anywhere, anywhere,
        ],
        out_specs=pl.BlockSpec(memory_space=pltpu.VMEM),
        scratch_shapes=[
            pltpu.VMEM(hidden_in.shape, bf16),
            pltpu.VMEM((blocks, HD), f32),
            pltpu.VMEM(cache_keys.shape, bf16),
            pltpu.VMEM(cache_values.shape, bf16),
            pltpu.VMEM((depth, columns), bf16),
            pltpu.VMEM((out_depth, out_columns), bf16),
            pltpu.VMEM((blocks, HD), f32),
            pltpu.VMEM((blocks, HD), bf16),
            pltpu.VMEM((PARTS, wide, blocks // PARTS, HD), bf16),
            pltpu.VMEM((wide * blocks // PARTS, HD), f32),
            pltpu.VMEM((wide, STEP), bf16),
            pltpu.VMEM((wide * narrow, 1, HD), f32),
            pltpu.VMEM((wide, heads, HD), f32),
            pltpu.VMEM((wide, heads, HD), f32),
            pltpu.VMEM((groups, share // groups * heads, HD), f32),
            pltpu.VMEM((mixed_blocks, HD), bf16),
            pltpu.VMEM((groups, wide, mixed_blocks // groups, HD), bf16),
            pltpu.VMEM((wide * mixed_blocks // groups, HD), f32),
            pltpu.VMEM((wide, out_depth // groups), bf16),
            pltpu.VMEM((PARTS, wide, out_blocks // PARTS, HD), f32),
            pltpu.VMEM((PARTS, wide, out_blocks // PARTS, HD), f32),
            dma((4,)), dma((depth // STEP,)), dma((out_depth // STEP,)),
            dma((1,)), dma((1,)),
            dma((PARTS,)), dma((PARTS,)),
            dma((1,)), dma((1,)),
            dma((groups,)), dma((groups,)),
            dma((PARTS,)), dma((PARTS,)),
        ],
        compiler_params=pltpu.CompilerParams(
            collective_id=0, has_side_effects=True,
            vmem_limit_bytes=63 * 1024 * 1024 + 768 * 1024,
        ),
        cost_estimate=pl.CostEstimate(
            flops=2 * wide * (depth * columns + out_depth * out_columns),
            bytes_accessed=2 * (depth * columns + out_depth * out_columns),
            transcendentals=0,
        ),
        name="decode",
    )(
        hidden_in, norm_gain.reshape(blocks, HD), cache_lengths,
        cache_keys, cache_values, qkv_weight, out_weight,
    )
    return out.reshape(1, blocks * HD)


def fits(sizes, hidden_in, qkv_weight, out_weight, cache_keys):
    wide, narrow = sizes
    columns = qkv_weight.shape[1]
    groups = cache_keys.shape[2] // HD
    if hidden_in.shape[0] != 1 or columns % HD or out_weight.shape[1] % (PARTS * 8 * HD):
        return False
    if wide % narrow or (wide // narrow) % groups or wide % 8:
        return False
    if qkv_weight.shape[0] % (PARTS * STEP) or out_weight.shape[0] % (groups * STEP):
        return False
    queries = (wide // narrow) // groups * (columns // HD) - 2
    return queries % 16 == 0 and queries * groups * HD == out_weight.shape[0]


def rotary(values, position):
    half = values.shape[-1] // 2
    frequency = rope_theta ** (-jnp.arange(half, dtype=jnp.float32) * 2.0 / values.shape[-1])
    angles = position[..., None] * frequency
    cosine = jnp.cos(angles)
    sine = jnp.sin(angles)
    first = values[..., :half]
    second = values[..., half:]
    return jnp.concatenate([first * cosine - second * sine, second * cosine + first * sine], -1)


def attend(joined, keys, values, lengths):
    count = joined.shape[0]
    groups = joined.shape[1]
    share = joined.shape[2] - 2
    head_dim = joined.shape[3]
    capacity = keys.shape[1]
    position = lengths.astype(jnp.float32)
    query = (rotary(joined[:, :, :share], position[:, None, None]) * head_dim ** (-0.5)).astype(
        jnp.bfloat16
    )
    new_key = rotary(joined[:, :, share], position[:, None]).astype(jnp.bfloat16)
    new_value = joined[:, :, share + 1].astype(jnp.bfloat16)
    keys_four = keys.reshape(count, capacity, groups, head_dim)
    values_four = values.reshape(count, capacity, groups, head_dim)
    scores = jnp.einsum("bgjd,btgd->bgjt", query, keys_four, preferred_element_type=jnp.float32)
    own = jnp.sum(query.astype(jnp.float32) * new_key.astype(jnp.float32)[:, :, None, :], -1)
    live = jnp.arange(capacity)[None, None, None, :] < lengths[:, None, None, None]
    scores = jnp.where(live, scores, -1e30)
    top = jnp.maximum(jnp.max(scores, -1), own)
    expo = jnp.exp(scores - top[..., None])
    own_expo = jnp.exp(own - top)
    total = jnp.sum(expo, -1) + own_expo
    probs = (expo / total[..., None]).astype(jnp.bfloat16)
    mixed = jnp.einsum("bgjt,btgd->bgjd", probs, values_four, preferred_element_type=jnp.float32)
    mixed = mixed + (own_expo / total)[..., None] * new_value.astype(jnp.float32)[:, :, None, :]
    return mixed.astype(jnp.bfloat16).reshape(count, groups * share * head_dim)


def body(hidden_in, norm_gain, qkv_weight, out_weight, cache_keys, cache_values, cache_lengths):
    sizes = [lax.axis_size(name) for name in ("wide", "narrow")]
    if fits(sizes, hidden_in, qkv_weight, out_weight, cache_keys):
        return fused(
            sizes, hidden_in, norm_gain, qkv_weight, out_weight,
            cache_keys, cache_values, cache_lengths,
        )
    inputs = hidden_in.astype(jnp.float32)
    row_count = hidden_in.shape[0]
    squares = lax.psum(jnp.sum(inputs * inputs, -1), "narrow")
    normed = (inputs * lax.rsqrt(squares / (hidden_in.shape[1] * sizes[1]) + norm_eps)[:, None] * norm_gain).astype(jnp.bfloat16)
    partial_qkv = jnp.dot(
        lax.all_gather(normed, "wide", axis=0, tiled=True),
        qkv_weight,
        preferred_element_type=jnp.float32,
    )
    all_rows, col_block = partial_qkv.shape
    halves = partial_qkv.reshape(all_rows, 1, 2, col_block // 2)
    paired = lax.psum_scatter(halves, "narrow", scatter_dimension=2, tiled=True)
    moved = lax.all_to_all(paired, "wide", split_axis=0, concat_axis=1, tiled=True)
    blocks = moved.shape[1]
    parted = moved.reshape(row_count, 2, blocks // 2, 1, col_block // 2)
    owned = lax.all_to_all(parted, "narrow", split_axis=1, concat_axis=3, tiled=True)
    owned = owned.reshape(row_count, blocks // 2 * col_block)
    groups = cache_keys.shape[2] // HD
    owned = owned.reshape(row_count, groups, owned.shape[1] // (groups * HD), HD)
    mixed = attend(owned, cache_keys, cache_values, cache_lengths)
    partial_out = jnp.dot(
        lax.all_gather(mixed, "wide", axis=0, tiled=True),
        out_weight,
        preferred_element_type=jnp.float32,
    )
    all_rows, col_block = partial_out.shape
    halves = partial_out.reshape(all_rows, 1, 2, col_block // 2)
    paired = lax.psum_scatter(halves, "narrow", scatter_dimension=2, tiled=True)
    moved = lax.all_to_all(paired, "wide", split_axis=0, concat_axis=1, tiled=True)
    blocks = moved.shape[1]
    parted = moved.reshape(row_count, 2, blocks // 2, 1, col_block // 2)
    added = lax.all_to_all(parted, "narrow", split_axis=1, concat_axis=3, tiled=True)
    added = added.reshape(row_count, blocks // 2 * col_block)
    return inputs + added


def solution(mesh):
    placed = (
        P(("group", "wide"), "narrow"),
        P("narrow"),
        P("narrow", "wide"),
        P("narrow", "wide"),
        P(("group", "wide"), None, "narrow"),
        P(("group", "wide"), None, "narrow"),
        P(("group", "wide")),
    )
    return jax.shard_map(
        body, mesh=mesh, in_specs=placed, out_specs=P(("group", "wide"), "narrow"), check_vma=False
    )
```

```python
import functools
import math

import jax
import jax.numpy as jnp
from jax import lax
from jax.experimental import pallas as pl
from jax.experimental.pallas import tpu as pltpu
from jax.sharding import PartitionSpec as P

HD = 128


rope_theta = 500000.0
norm_eps = 1e-05
MESH = pl.DeviceIdType.MESH


PARTS = 2
PIECE = 1024
STEP = 2048


def decode_kernel(
    wide, narrow, heads, groups, features,
    h_hbm, g_hbm, len_ref, k_hbm, v_hbm, wq_hbm, wo_hbm, out_ref,
    h_in, gain, keys, values, wq, wo, hf, hsend, hrec, xs, lhs, ssrec, psend, prec, joined,
    msend, mrec, ms, lhs2, osend, orec,
    in_sem, q_sem, w_sem, ss_s, ss_r, h_s, h_r, p_s, p_r, m_s, m_r, o_s, o_r,
):
    w = lax.axis_index("wide")
    n = lax.axis_index("narrow")
    share = wide // narrow
    blocks = hf.shape[0]
    depth, out_depth = wq.shape[0], wo.shape[0]
    turns = [w] + [lax.rem(w + d, wide) for d in range(1, wide)]

    def load(weights, held, sem, step):
        for i in range(STEP // PIECE):
            at = pl.ds(step * STEP + i * PIECE, PIECE)
            pltpu.make_async_copy(weights.at[at, :], held.at[at, :], sem.at[step]).start()

    def loaded(held, sem, step):
        block = held.at[pl.ds(step * STEP, STEP), :]
        pltpu.make_async_copy(block, block, sem.at[step]).wait()

    h_copy = pltpu.make_async_copy(h_hbm, h_in, in_sem.at[0])
    g_copy = pltpu.make_async_copy(g_hbm, gain, in_sem.at[1])
    k_copy = pltpu.make_async_copy(k_hbm, keys, in_sem.at[2])
    v_copy = pltpu.make_async_copy(v_hbm, values, in_sem.at[3])
    h_copy.start()
    g_copy.start()

    barrier = pltpu.get_barrier_semaphore()
    for d in range(wide):
        for e in range(narrow):
            if d or e:
                pl.semaphore_signal(
                    barrier, inc=1,
                    device_id={"wide": turns[d], "narrow": lax.rem(n + e, narrow)},
                    device_id_type=MESH,
                )

    for step in range(depth // STEP):
        load(wq_hbm, wq, q_sem, step)

    h_copy.wait()
    wide_row = h_in[...].astype(jnp.float32)
    for b in range(blocks):
        hf[b : b + 1, :] = wide_row[:, b * HD : (b + 1) * HD]
    own = hf[...]
    squares = jnp.sum(own * own, axis=0, keepdims=True)
    me = n * wide + w
    ssrec[me] = squares
    hsend[...] = own.astype(jnp.bfloat16)
    g_copy.wait()

    pl.semaphore_wait(barrier, wide * narrow - 1)

    def spread(source, target, part, send, recv):
        size = target.shape[2]
        block = source.at[pl.ds(part * size, size)]
        for d in range(1, wide):
            pltpu.make_async_remote_copy(
                src_ref=block, dst_ref=target.at[part, w],
                send_sem=send.at[part], recv_sem=recv.at[part],
                device_id={"wide": turns[d]},
                device_id_type=MESH,
            ).start()
        target[part, w] = block[...]

    def wait_for(buffer, count, sem):
        block = buffer.at[pl.ds(0, count)]
        pltpu.make_async_copy(block, block, sem).wait()

    for d in range(wide):
        for e in range(narrow):
            if d or e:
                pltpu.make_async_remote_copy(
                    src_ref=ssrec.at[me], dst_ref=ssrec.at[me],
                    send_sem=ss_s.at[0], recv_sem=ss_r.at[0],
                    device_id={"wide": turns[d], "narrow": lax.rem(n + e, narrow)},
                    device_id_type=MESH,
                ).start()
    for part in range(PARTS):
        spread(hsend, hrec, part, h_s, h_r)
    k_copy.start()
    v_copy.start()
    position = len_ref[0].astype(jnp.float32)
    lane = lax.broadcasted_iota(jnp.int32, (1, HD), 1)
    turn = lax.rem(lane, HD // 2).astype(jnp.float32)
    angles = position * jnp.exp(turn * (-2.0 / HD * math.log(rope_theta)))
    cosine = jnp.cos(angles)
    sine = jnp.where(lane < HD // 2, -jnp.sin(angles), jnp.sin(angles))

    wait_for(ssrec, wide * narrow - 1, ss_r.at[0])
    squares = ssrec[0:wide]
    for part in range(1, narrow):
        squares = squares + ssrec[part * wide : (part + 1) * wide]
    scale = lax.rsqrt(jnp.sum(squares, axis=-1, keepdims=True) / features + norm_eps)
    per = STEP // HD
    half = blocks // PARTS
    total = None
    for part in range(PARTS):
        wait_for(hrec.at[part], wide - 1, h_r.at[part])
        gains = gain[part * half : (part + 1) * half, :]
        for s in range(wide):
            xs[s * half : (s + 1) * half, :] = hrec[part, s].astype(jnp.float32) * scale[s] * gains
        for step in range(half // per):
            for b in range(per):
                lhs[:, b * HD : (b + 1) * HD] = xs[
                    pl.ds(step * per + b, wide, stride=half), :
                ].astype(jnp.bfloat16)
            at = part * (half // per) + step
            loaded(wq, q_sem, at)
            if at == depth // STEP - 1:
                for later in range(out_depth // STEP):
                    load(wo_hbm, wo, w_sem, later)
            product = jnp.dot(
                lhs[...], wq[at * STEP : (at + 1) * STEP, :], preferred_element_type=jnp.float32
            )
            total = product if total is None else total + product
    for j in range(heads):
        psend[:, j, :] = total[:, j * HD : (j + 1) * HD]

    slot = lax.rem(w, share) * narrow + n
    owner = w // share

    def collect(source, target, send, recv):
        for d in range(wide):
            copy = pltpu.make_async_remote_copy(
                src_ref=source.at[turns[d]], dst_ref=target.at[slot],
                send_sem=send, recv_sem=recv,
                device_id={"wide": turns[d], "narrow": owner},
                device_id_type=MESH,
            )
            if d:
                copy.start()
                continue

            @pl.when(owner == n)
            def _():
                pltpu.make_async_copy(source.at[w], target.at[slot], recv).start()

            @pl.when(owner != n)
            def _():
                copy.start()

    def added(target, b):
        block = target[b * narrow]
        for i in range(1, narrow):
            block = block + target[b * narrow + i]
        return block

    collect(psend, prec, p_s.at[0], p_r.at[0])
    k_copy.wait()
    v_copy.wait()
    wait_for(prec, wide, p_r.at[0])

    per_group = share // groups
    context = keys.shape[1]
    queries = per_group * heads - 2
    for g in range(groups):
        for b in range(per_group):
            joined[g, b * heads : (b + 1) * heads, :] = added(prec, g * per_group + b)
    for g in range(groups):
        turned = joined[g, 0 : queries, :]
        turned = turned * cosine + pltpu.roll(turned, HD // 2, 1) * sine
        query = (turned * HD ** (-0.5)).astype(jnp.bfloat16)
        new_key = joined[g, queries : queries + 1, :]
        new_key = new_key * cosine + pltpu.roll(new_key, HD // 2, 1) * sine
        new_key = new_key.astype(jnp.bfloat16).astype(jnp.float32)
        new_value = joined[g, queries + 1 : queries + 2, :].astype(jnp.bfloat16).astype(jnp.float32)
        scores = lax.dot_general(
            query, keys[0, :, g * HD : (g + 1) * HD], (((1,), (1,)), ((), ())),
            preferred_element_type=jnp.float32,
        )
        own_score = jnp.sum(query.astype(jnp.float32) * new_key, axis=-1, keepdims=True)
        live = lax.broadcasted_iota(jnp.int32, (queries, context), 1) < len_ref[0]
        scores = jnp.where(live, scores, -1e30)
        top = jnp.maximum(jnp.max(scores, axis=-1, keepdims=True), own_score)
        expo = jnp.exp(scores - top)
        own_expo = jnp.exp(own_score - top)
        weight = jnp.sum(expo, axis=-1, keepdims=True) + own_expo
        probs = (expo / weight).astype(jnp.bfloat16)
        mixed = jnp.dot(
            probs, values[0, :, g * HD : (g + 1) * HD], preferred_element_type=jnp.float32
        )
        mixed = mixed + (own_expo / weight) * new_value
        msend[g * queries : (g + 1) * queries, :] = mixed.astype(jnp.bfloat16)
        spread(msend, mrec, g, m_s, m_r)

    deep = queries * HD
    width = wo.shape[1] // PARTS
    count = width // HD
    total = None
    for g in range(groups):
        wait_for(mrec.at[g], wide - 1, m_r.at[g])
        for s in range(wide):
            ms[s * queries : (s + 1) * queries, :] = mrec[g, s].astype(jnp.float32)
        for b in range(queries):
            lhs2[:, b * HD : (b + 1) * HD] = ms[
                pl.ds(b, wide, stride=queries), :
            ].astype(jnp.bfloat16)
        for step in range(g * deep // STEP, (g + 1) * deep // STEP):
            loaded(wo, w_sem, step)
        if g < groups - 1:
            product = jnp.dot(
                lhs2[...], wo[g * deep : (g + 1) * deep, :], preferred_element_type=jnp.float32
            )
            total = product if total is None else total + product
            continue
        for part in range(PARTS):
            at = slice(part * width, (part + 1) * width)
            product = jnp.dot(
                lhs2[...], wo[g * deep : (g + 1) * deep, at], preferred_element_type=jnp.float32
            )
            if total is not None:
                product = total[:, at] + product
            for j in range(count):
                osend[part, :, j, :] = product[:, j * HD : (j + 1) * HD]
            collect(osend.at[part], orec.at[part], o_s.at[part], o_r.at[part])

    for part in range(PARTS):
        wait_for(orec.at[part], wide, o_r.at[part])
        for b in range(share):
            start = (b * PARTS + part) * count
            out_ref[start : start + count, :] = hf[start : start + count, :] + added(orec.at[part], b)

    wait_for(ssrec, wide * narrow - 1, ss_s.at[0])
    sent = [(hrec.at[part], h_s.at[part]) for part in range(PARTS)]
    sent += [(mrec.at[g], m_s.at[g]) for g in range(groups)]
    shared = [(prec, p_s.at[0])]
    shared += [(orec.at[part], o_s.at[part]) for part in range(PARTS)]
    for buffer, sem in sent + shared:
        wait_for(buffer, wide - 1, sem)

    @pl.when(owner != n)
    def _():
        for buffer, sem in shared:
            wait_for(buffer, 1, sem)


def fused(sizes, hidden_in, norm_gain, qkv_weight, out_weight, cache_keys, cache_values, cache_lengths):
    wide, narrow = sizes
    depth, columns = qkv_weight.shape
    out_depth, out_columns = out_weight.shape
    heads = columns // HD
    groups = cache_keys.shape[2] // HD
    blocks = depth // HD
    out_blocks = out_columns // HD
    share = wide // narrow
    mixed_blocks = out_depth // HD
    bf16, f32 = jnp.bfloat16, jnp.float32
    dma = pltpu.SemaphoreType.DMA
    anywhere = pl.BlockSpec(memory_space=pltpu.HBM)
    out = pl.pallas_call(
        functools.partial(decode_kernel, wide, narrow, heads, groups, depth * narrow),
        out_shape=jax.ShapeDtypeStruct((blocks, HD), f32),
        in_specs=[
            anywhere, anywhere, pl.BlockSpec(memory_space=pltpu.SMEM),
            anywhere, anywhere, anywhere, anywhere,
        ],
        out_specs=pl.BlockSpec(memory_space=pltpu.VMEM),
        scratch_shapes=[
            pltpu.VMEM(hidden_in.shape, bf16),
            pltpu.VMEM((blocks, HD), f32),
            pltpu.VMEM(cache_keys.shape, bf16),
            pltpu.VMEM(cache_values.shape, bf16),
            pltpu.VMEM((depth, columns), bf16),
            pltpu.VMEM((out_depth, out_columns), bf16),
            pltpu.VMEM((blocks, HD), f32),
            pltpu.VMEM((blocks, HD), bf16),
            pltpu.VMEM((PARTS, wide, blocks // PARTS, HD), bf16),
            pltpu.VMEM((wide * blocks // PARTS, HD), f32),
            pltpu.VMEM((wide, STEP), bf16),
            pltpu.VMEM((wide * narrow, 1, HD), f32),
            pltpu.VMEM((wide, heads, HD), f32),
            pltpu.VMEM((wide, heads, HD), f32),
            pltpu.VMEM((groups, share // groups * heads, HD), f32),
            pltpu.VMEM((mixed_blocks, HD), bf16),
            pltpu.VMEM((groups, wide, mixed_blocks // groups, HD), bf16),
            pltpu.VMEM((wide * mixed_blocks // groups, HD), f32),
            pltpu.VMEM((wide, out_depth // groups), bf16),
            pltpu.VMEM((PARTS, wide, out_blocks // PARTS, HD), f32),
            pltpu.VMEM((PARTS, wide, out_blocks // PARTS, HD), f32),
            dma((4,)), dma((depth // STEP,)), dma((out_depth // STEP,)),
            dma((1,)), dma((1,)),
            dma((PARTS,)), dma((PARTS,)),
            dma((1,)), dma((1,)),
            dma((groups,)), dma((groups,)),
            dma((PARTS,)), dma((PARTS,)),
        ],
        compiler_params=pltpu.CompilerParams(
            collective_id=0, has_side_effects=True,
            vmem_limit_bytes=63 * 1024 * 1024 + 768 * 1024,
        ),
        cost_estimate=pl.CostEstimate(
            flops=2 * wide * (depth * columns + out_depth * out_columns),
            bytes_accessed=2 * (depth * columns + out_depth * out_columns),
            transcendentals=0,
        ),
        name="decode",
    )(
        hidden_in, norm_gain.reshape(blocks, HD), cache_lengths,
        cache_keys, cache_values, qkv_weight, out_weight,
    )
    return out.reshape(1, blocks * HD)


def fits(sizes, hidden_in, qkv_weight, out_weight, cache_keys):
    wide, narrow = sizes
    columns = qkv_weight.shape[1]
    groups = cache_keys.shape[2] // HD
    if hidden_in.shape[0] != 1 or columns % HD or out_weight.shape[1] % (PARTS * 8 * HD):
        return False
    if wide % narrow or (wide // narrow) % groups or wide % 8:
        return False
    if qkv_weight.shape[0] % (PARTS * STEP) or out_weight.shape[0] % (groups * STEP):
        return False
    queries = (wide // narrow) // groups * (columns // HD) - 2
    return queries % 16 == 0 and queries * groups * HD == out_weight.shape[0]


def rotary(values, position):
    half = values.shape[-1] // 2
    frequency = rope_theta ** (-jnp.arange(half, dtype=jnp.float32) * 2.0 / values.shape[-1])
    angles = position[..., None] * frequency
    cosine = jnp.cos(angles)
    sine = jnp.sin(angles)
    first = values[..., :half]
    second = values[..., half:]
    return jnp.concatenate([first * cosine - second * sine, second * cosine + first * sine], -1)


def attend(joined, keys, values, lengths):
    count = joined.shape[0]
    groups = joined.shape[1]
    share = joined.shape[2] - 2
    head_dim = joined.shape[3]
    capacity = keys.shape[1]
    position = lengths.astype(jnp.float32)
    query = (rotary(joined[:, :, :share], position[:, None, None]) * head_dim ** (-0.5)).astype(
        jnp.bfloat16
    )
    new_key = rotary(joined[:, :, share], position[:, None]).astype(jnp.bfloat16)
    new_value = joined[:, :, share + 1].astype(jnp.bfloat16)
    keys_four = keys.reshape(count, capacity, groups, head_dim)
    values_four = values.reshape(count, capacity, groups, head_dim)
    scores = jnp.einsum("bgjd,btgd->bgjt", query, keys_four, preferred_element_type=jnp.float32)
    own = jnp.sum(query.astype(jnp.float32) * new_key.astype(jnp.float32)[:, :, None, :], -1)
    live = jnp.arange(capacity)[None, None, None, :] < lengths[:, None, None, None]
    scores = jnp.where(live, scores, -1e30)
    top = jnp.maximum(jnp.max(scores, -1), own)
    expo = jnp.exp(scores - top[..., None])
    own_expo = jnp.exp(own - top)
    total = jnp.sum(expo, -1) + own_expo
    probs = (expo / total[..., None]).astype(jnp.bfloat16)
    mixed = jnp.einsum("bgjt,btgd->bgjd", probs, values_four, preferred_element_type=jnp.float32)
    mixed = mixed + (own_expo / total)[..., None] * new_value.astype(jnp.float32)[:, :, None, :]
    return mixed.astype(jnp.bfloat16).reshape(count, groups * share * head_dim)


def body(hidden_in, norm_gain, qkv_weight, out_weight, cache_keys, cache_values, cache_lengths):
    sizes = [lax.axis_size(name) for name in ("wide", "narrow")]
    if fits(sizes, hidden_in, qkv_weight, out_weight, cache_keys):
        return fused(
            sizes, hidden_in, norm_gain, qkv_weight, out_weight,
            cache_keys, cache_values, cache_lengths,
        )
    inputs = hidden_in.astype(jnp.float32)
    row_count = hidden_in.shape[0]
    squares = lax.psum(jnp.sum(inputs * inputs, -1), "narrow")
    normed = (inputs * lax.rsqrt(squares / (hidden_in.shape[1] * sizes[1]) + norm_eps)[:, None] * norm_gain).astype(jnp.bfloat16)
    partial_qkv = jnp.dot(
        lax.all_gather(normed, "wide", axis=0, tiled=True),
        qkv_weight,
        preferred_element_type=jnp.float32,
    )
    all_rows, col_block = partial_qkv.shape
    halves = partial_qkv.reshape(all_rows, 1, 2, col_block // 2)
    paired = lax.psum_scatter(halves, "narrow", scatter_dimension=2, tiled=True)
    moved = lax.all_to_all(paired, "wide", split_axis=0, concat_axis=1, tiled=True)
    blocks = moved.shape[1]
    parted = moved.reshape(row_count, 2, blocks // 2, 1, col_block // 2)
    owned = lax.all_to_all(parted, "narrow", split_axis=1, concat_axis=3, tiled=True)
    owned = owned.reshape(row_count, blocks // 2 * col_block)
    groups = cache_keys.shape[2] // HD
    owned = owned.reshape(row_count, groups, owned.shape[1] // (groups * HD), HD)
    mixed = attend(owned, cache_keys, cache_values, cache_lengths)
    partial_out = jnp.dot(
        lax.all_gather(mixed, "wide", axis=0, tiled=True),
        out_weight,
        preferred_element_type=jnp.float32,
    )
    all_rows, col_block = partial_out.shape
    halves = partial_out.reshape(all_rows, 1, 2, col_block // 2)
    paired = lax.psum_scatter(halves, "narrow", scatter_dimension=2, tiled=True)
    moved = lax.all_to_all(paired, "wide", split_axis=0, concat_axis=1, tiled=True)
    blocks = moved.shape[1]
    parted = moved.reshape(row_count, 2, blocks // 2, 1, col_block // 2)
    added = lax.all_to_all(parted, "narrow", split_axis=1, concat_axis=3, tiled=True)
    added = added.reshape(row_count, blocks // 2 * col_block)
    return inputs + added


def solution(mesh):
    placed = (
        P(("group", "wide"), "narrow"),
        P("narrow"),
        P("narrow", "wide"),
        P("narrow", "wide"),
        P(("group", "wide"), None, "narrow"),
        P(("group", "wide"), None, "narrow"),
        P(("group", "wide")),
    )
    return jax.shard_map(
        body, mesh=mesh, in_specs=placed, out_specs=P(("group", "wide"), "narrow"), check_vma=False
    )
```
